32 devices in a mesh: section: 4 (over x, core), tensor: 8 (over z, y).
Axes of the slice: x: 2, y: 2, z: 4, core: 2. Of those that a mesh axis runs over, the one named last changes fastest.
Arguments:
- context: bfloat16 [4, 256, 1024], P('section', None, 'tensor'), may hold values from -6 to 6
- out_weight: bfloat16 [4, 1024, 8192], P('section', 'tensor'), may hold values from -0.1875 to 0.1875
- residual: bfloat16 [4, 256, 8192], P('section', None, 'tensor'), may hold values from -36 to 36
- gain: float32 [4, 8192], P('section', 'tensor'), may hold values from 0.1 to 1.9
- q_weight: bfloat16 [4, 8192, 1024], P('section', None, 'tensor'), may hold values from -0.044194174 to 0.044194174
- kv_weight: bfloat16 [4, 8192, 256], P('section', None, 'tensor'), may hold values from -0.044194174 to 0.044194174
Outputs:
- attended: bfloat16 [4, 256, 1024], P('section', None, 'tensor')
The draws below stay inside these ranges and needn't reach their ends.
All inputs are finite; a program needn't handle non-finite values.
Results may differ from the reference program's by a relative error of at most 0.033.
Values may be sent and summed in bfloat16 or wider, within the bound.
A program may use at most 64 MiB of HBM per device.

```python
import jax
import jax.numpy as jnp
from jax import lax

D = 8192
HD = 128
GROUP = 8
SEQ = 256
HEADS = 8
KV_HEADS = 1
N_SECTION = 4
N_TENSOR = 8


def draw_residual(key, part):
    values = jnp.clip(jax.random.normal(key, (N_SECTION, SEQ, D), jnp.float32), -4.0, 4.0)
    position = jnp.arange(D).astype(jnp.float32) / D
    rising = 3.0 ** position
    return (values * rising[None, None, :]).astype(jnp.bfloat16)


def draw_q_weight(key, part):
    values = jnp.clip(jax.random.normal(key, (N_SECTION, D, HEADS * HD), jnp.float32), -4.0, 4.0)
    return (values * D ** (-0.5)).astype(jnp.bfloat16)


def draw_kv_weight(key, part):
    values = jnp.clip(jax.random.normal(key, (N_SECTION, D, 2 * HD * KV_HEADS), jnp.float32), -4.0, 4.0)
    return (values * D ** (-0.5)).astype(jnp.bfloat16)


def steps_of(stream_key, shape, split, smallest, top_value):
    def one(dim, blocks):
        heights = jax.random.uniform(jax.random.fold_in(jax.random.fold_in(stream_key, 6), dim), (blocks,), jnp.float32, smallest / len(split), top_value / len(split))
        return jnp.repeat(jnp.exp(heights), shape[dim] // blocks).reshape((-1,) + (1,) * (len(shape) - dim - 1))

    factor_of = one(*split[0])
    for cut in split[1:]:
        factor_of = factor_of * one(*cut)
    return factor_of


def gaussian(stream_key, extent, spread, most, shards=(), dtype=jnp.bfloat16):
    array = spread * jax.random.normal(stream_key, extent, jnp.float32)
    if shards:
        array = array * steps_of(stream_key, extent, shards, -0.22, 0.18)
    return jnp.clip(array, -most, most).astype(dtype)


def setup_inputs(seed: int = 0) -> dict:
    splits = jax.random.split(jax.random.key(seed), 7)
    context = gaussian(splits[0], (N_SECTION, SEQ, HEADS * HD), 1.0, 6.0, ((0, 4), (2, 8)))
    out_weight = gaussian(splits[1], (N_SECTION, HEADS * HD, D), (HEADS * HD) ** -0.5, 0.1875, ((0, 4), (1, 8)))
    residual = draw_residual(jax.random.fold_in(splits[6], 71), 0)
    gain = jnp.clip(1.0 + 0.18 * jax.random.normal(splits[3], (N_SECTION, D), jnp.float32), 0.1, 1.9)
    q_weight = draw_q_weight(jax.random.fold_in(splits[6], 71), 0)
    kv_weight = draw_kv_weight(jax.random.fold_in(splits[6], 71), 0)
    return dict(context=context, out_weight=out_weight, residual=residual, gain=gain, q_weight=q_weight, kv_weight=kv_weight)


THETA = 500000.0

def rotate(inputs, positions):
    half_width = inputs.shape[-1] // 2
    frequency = THETA ** (-(jnp.arange(half_width).astype(jnp.float32) * 2.0 / inputs.shape[-1]))
    angles = positions[:, None] * frequency[None, :]
    cosine = jnp.cos(angles)[:, None, :]
    sine_part = jnp.sin(angles)[:, None, :]
    first_half = inputs[..., :half_width]
    second_half = inputs[..., half_width:]
    return jnp.concatenate([first_half * cosine - second_half * sine_part, second_half * cosine + first_half * sine_part], axis=-1)

def reference(context, out_weight, residual, gain, q_weight, kv_weight):

    def send_section(inputs):
        local_context, local_out, local_residual = inputs

        def add_head(running, head_index):
            block_cols = lax.dynamic_slice_in_dim(local_context, head_index * HD, HD, 1)
            block_rows = lax.dynamic_slice_in_dim(local_out, head_index * HD, HD, 0)
            head_term = jnp.dot(block_cols, block_rows, preferred_element_type=jnp.float32).astype(jnp.bfloat16)
            head_term = lax.optimization_barrier(head_term)
            return (running + head_term.astype(jnp.float32), None)
        running, _ = lax.scan(add_head, jnp.zeros((SEQ, D), jnp.float32), jnp.arange(HEADS).astype(jnp.int32))
        return (local_residual.astype(jnp.float32) + running).astype(jnp.bfloat16)
    handover = lax.map(send_section, (context, out_weight, residual))
    received = jnp.roll(handover, 1, axis=0)
    positions = jnp.arange(SEQ).astype(jnp.float32)
    order = jnp.arange(SEQ)
    causal = order[:, None] >= order[None, :]
    feature_share = HD // N_TENSOR

    def receive(inputs):
        arriving, section_gain, query_cols, pair_cols = inputs
        values_f = arriving.astype(jnp.float32)
        normed = (values_f * lax.rsqrt(lax.optimization_barrier(jnp.mean(values_f * values_f, axis=-1, keepdims=True)) + 1e-05) * section_gain[None, :]).astype(jnp.bfloat16)
        queries = jnp.dot(normed, query_cols, preferred_element_type=jnp.float32).reshape(SEQ, HEADS, HD)
        queries = rotate(queries, positions).astype(jnp.bfloat16)
        pair_proj = jnp.dot(normed, pair_cols, preferred_element_type=jnp.float32).astype(jnp.bfloat16)
        pair_proj = pair_proj.reshape(SEQ, N_TENSOR, KV_HEADS, 2, feature_share)
        pair_proj = jnp.transpose(pair_proj, (0, 2, 3, 1, 4)).reshape(SEQ, KV_HEADS, 2, HD)
        keys = rotate(pair_proj[:, :, 0].astype(jnp.float32), positions).astype(jnp.bfloat16)
        values = pair_proj[:, :, 1]
        grouped = queries.reshape(SEQ, KV_HEADS, GROUP, HD).astype(jnp.float32)
        scores = jnp.einsum('sghd,tgd->ghst', grouped, keys.astype(jnp.float32)) * HD ** (-0.5)
        scores = jnp.where(causal[None, None], scores, -1e+30)
        softmax_weights = jax.nn.softmax(scores, axis=-1).astype(jnp.bfloat16)
        attended = jnp.einsum('ghst,tgd->sghd', softmax_weights.astype(jnp.float32), values.astype(jnp.float32))
        return attended.astype(jnp.bfloat16).reshape(SEQ, HEADS * HD)
    return lax.map(receive, (received, gain, q_weight, kv_weight))
```

```python
import functools

import jax
import jax.numpy as jnp
import numpy as np
from jax import lax
from jax.experimental import pallas as pl
from jax.experimental.pallas import tpu as pltpu
from jax.sharding import PartitionSpec as P

GROUP = 8
THETA = 500000.0
EPS = 1e-05
MESH = pl.DeviceIdType.MESH
BF16 = jnp.bfloat16
F32 = jnp.float32
NG = 4


def rope_tables(length, head_size):
    half = head_size // 2
    frequency = np.float32(THETA) ** (-(np.arange(half, dtype=np.float32) * np.float32(2.0) / np.float32(head_size)))
    angles = np.arange(length, dtype=np.float32)[:, None] * frequency.astype(np.float32)[None, :]
    cosine, sine = np.cos(angles).astype(np.float32), np.sin(angles).astype(np.float32)
    return (
        np.concatenate([cosine, cosine], axis=1),
        np.concatenate([-sine, sine], axis=1),
        np.ascontiguousarray(np.concatenate([cosine, cosine], axis=1).T),
        np.ascontiguousarray(np.concatenate([-sine, sine], axis=1).T),
    )


def dot_nt(a, b):
    return lax.dot_general(a, b, (((1,), (1,)), ((), ())), preferred_element_type=F32)


def kernel(
    T, S,
    ctx, res, gain, cos_q, sin_q, cos_k, sin_k, ow_hbm, qw_hbm, kvw_hbm,
    out,
    ow, kvw, w, first, rs, hand, xb, gains, acc, ssq, kvall,
    load_sem, rs_send, rs_recv, sh_send, sh_recv, ag_send, ag_recv, g_send, g_recv, kv_send, kv_recv,
):
    L, HD = ctx.shape
    B = res.shape[1]
    D = ow.shape[1]
    KC = kvw.shape[1]
    R = L // NG
    half = L // 2
    sec = lax.axis_index("section")
    me = lax.axis_index("tensor")

    def ring(pos):
        upper = pos // (T // 2)
        return (1 - upper) * (2 * pos) + upper * (2 * (T - 1 - pos) + 1)

    y = me % 2
    p = (1 - y) * (me // 2) + y * (T - 1 - me // 2)

    def at(offset):
        return ring((p + offset + 2 * T) % T)

    sides = (at(1), at(-1))
    signs = (1, -1)
    side_of = [0 if g < NG // 2 else 1 for g in range(NG)]
    following = (sec + 1) % S
    previous = (sec + S - 1) % S

    loads = [
        pltpu.make_async_copy(ow_hbm, ow, load_sem.at[0]),
        pltpu.make_async_copy(kvw_hbm, kvw, load_sem.at[1]),
        pltpu.make_async_copy(qw_hbm, w.at[:, pl.ds(0, HD)], load_sem.at[2]),
    ]
    for load in loads:
        load.start()

    barrier = pltpu.get_barrier_semaphore()

    def greet(j, c):
        pl.semaphore_signal(barrier, inc=1, device_id=(sec, (me + j) % T), device_id_type=MESH)
        return c

    lax.fori_loop(1, T, greet, 0)
    pl.semaphore_signal(barrier, inc=1, device_id=(following, me), device_id_type=MESH)
    pl.semaphore_signal(barrier, inc=1, device_id=(previous, me), device_id_type=MESH)
    pl.semaphore_wait(barrier, T + 1)

    def rows(g):
        return pl.ds(g * R, R)

    def rs_copy(g, k, source):
        return pltpu.make_async_remote_copy(
            src_ref=source, dst_ref=rs.at[g, k], send_sem=rs_send.at[g, k], recv_sem=rs_recv.at[g, k],
            device_id=(sec, sides[side_of[g]]), device_id_type=MESH,
        )

    def shift_copy(g):
        return pltpu.make_async_remote_copy(
            src_ref=hand.at[rows(g)], dst_ref=xb.at[me, rows(g)], send_sem=sh_send.at[g], recv_sem=sh_recv.at[g],
            device_id=(following, me), device_id_type=MESH,
        )

    def ag_copy(g, k, owner):
        return pltpu.make_async_remote_copy(
            src_ref=xb.at[owner, rows(g)], dst_ref=xb.at[owner, rows(g)],
            send_sem=ag_send.at[g, k], recv_sem=ag_recv.at[g, k],
            device_id=(sec, sides[side_of[g]]), device_id_type=MESH,
        )

    def gain_copy(peer, slot):
        return pltpu.make_async_remote_copy(
            src_ref=gain, dst_ref=gains.at[slot], send_sem=g_send.at[peer], recv_sem=g_recv.at[slot],
            device_id=(sec, peer), device_id_type=MESH,
        )

    def kv_copy(peer, slot):
        return pltpu.make_async_remote_copy(
            src_ref=kvall.at[me], dst_ref=kvall.at[slot], send_sem=kv_send.at[peer], recv_sem=kv_recv.at[slot],
            device_id=(sec, peer), device_id_type=MESH,
        )

    def each_peer(act):
        def step(j, c):
            act((me + j) % T)
            return c

        lax.fori_loop(1, T, step, 0)

    def term(side, owner):
        return jnp.dot(
            ctx[pl.ds(side * half, half), :],
            ow[:, pl.ds(pl.multiple_of(owner * B, B), B)],
            preferred_element_type=F32,
        )

    loads[0].wait()
    for side in range(2):
        part = term(side, at(-signs[side])).astype(BF16)
        for g in range(NG):
            if side_of[g] == side:
                start = g * R - side * half
                first[g] = part[start:start + R]
                rs_copy(g, 0, first.at[g]).start()

    gains[me] = gain[...]
    each_peer(lambda peer: gain_copy(peer, me).start())

    loads[1].wait()
    CH = 512

    def place(i, c):
        at_rows = pl.ds(pl.multiple_of(i * CH, CH), CH)
        w[at_rows, HD:] = jnp.concatenate([kvw[at_rows, :], jnp.zeros((CH, HD - KC), BF16)], axis=1)
        return c

    lax.fori_loop(0, D // CH, place, 0)

    def reduce_step(k, c):
        parts = [term(side, at(-signs[side] * (2 + k))) for side in range(2)]
        for j in range(NG // 2):
            for g in (j, j + NG // 2):
                start = j * R
                rs_copy(g, k, first.at[g]).wait_recv()
                rs[g, k] = (rs[g, k].astype(F32) + parts[side_of[g]][start:start + R]).astype(BF16)
                rs_copy(g, k + 1, rs.at[g, k]).start()
        return c

    lax.fori_loop(0, T - 2, reduce_step, 0)

    parts = [term(side, me) for side in range(2)]
    for j in range(NG // 2):
        for g in (j, j + NG // 2):
            rs_copy(g, T - 2, first.at[g]).wait_recv()
            total = rs[g, T - 2].astype(F32) + parts[side_of[g]][j * R:j * R + R]
            hand[rows(g), :] = (res[rows(g), :].astype(F32) + total).astype(BF16)
            shift_copy(g).start()

    for j in range(NG // 2):
        for g in (j, j + NG // 2):
            shift_copy(g).wait_recv()
            ag_copy(g, 0, me).start()

    each_peer(lambda peer: gain_copy(peer, peer).wait_recv())
    loads[2].wait()
    acc[...] = jnp.zeros_like(acc)
    ssq[...] = jnp.zeros_like(ssq)
    ones = jnp.ones((B, HD), BF16)

    def project(side, owner):
        at_rows = pl.ds(side * half, half)
        block = xb[owner, at_rows, :].astype(F32)
        scaled = (block * gains[owner]).astype(BF16)
        squares = (block * block).astype(BF16)
        acc[at_rows, :] += jnp.dot(
            scaled, w[pl.ds(pl.multiple_of(owner * B, B), B), :], preferred_element_type=F32
        )
        ssq[at_rows, :] += jnp.dot(squares, ones, preferred_element_type=F32)

    for side in range(2):
        project(side, me)

    def gather_step(k, c):
        owners = [at(-signs[side] * (1 + k)) for side in range(2)]
        for j in range(NG // 2):
            for g in (j, j + NG // 2):
                ag_copy(g, k, owners[side_of[g]]).wait_recv()
                ag_copy(g, k + 1, owners[side_of[g]]).start()
        for side in range(2):
            project(side, owners[side])
        return c

    lax.fori_loop(0, T - 2, gather_step, 0)
    owners = [at(-signs[side] * (T - 1)) for side in range(2)]
    for j in range(NG // 2):
        for g in (j, j + NG // 2):
            ag_copy(g, T - 2, owners[side_of[g]]).wait_recv()
    for side in range(2):
        project(side, owners[side])

    factor = lax.rsqrt(ssq[...] * (1.0 / D) + EPS)
    pairs = (acc[:, HD:] * factor).astype(BF16)
    picks = lax.broadcasted_iota(jnp.int32, (KC, HD), 0) == lax.broadcasted_iota(jnp.int32, (KC, HD), 1)
    kvall[me] = dot_nt(picks.astype(F32).astype(BF16), pairs).astype(BF16)
    each_peer(lambda peer: kv_copy(peer, me).start())

    queries = acc[:, :HD] * factor
    turned = jnp.concatenate([queries[:, HD // 2:], queries[:, :HD // 2]], axis=1)
    queries = (queries * cos_q[...] + turned * sin_q[...]).astype(BF16)

    share = HD // T
    shift = share.bit_length() - 1
    feature = lax.broadcasted_iota(jnp.int32, (HD, T * KC), 0)
    column = lax.broadcasted_iota(jnp.int32, (HD, T * KC), 1)
    source = (feature >> shift) * KC + (feature & (share - 1)) + (me // GROUP) * (2 * share)
    key_picks = (column == source).astype(F32).astype(BF16)
    value_picks = (column == source + share).astype(F32).astype(BF16)

    each_peer(lambda peer: kv_copy(peer, peer).wait_recv())
    everything = kvall[...].reshape(T * KC, L)
    keys = jnp.dot(key_picks, everything, preferred_element_type=F32)
    values = jnp.dot(value_picks, everything, preferred_element_type=F32).astype(BF16)
    turned = jnp.concatenate([keys[HD // 2:], keys[:HD // 2]], axis=0)
    keys = (keys * cos_k[...] + turned * sin_k[...]).astype(BF16)
    scores = jnp.dot(queries, keys, preferred_element_type=F32) * (HD ** -0.5)
    before = lax.broadcasted_iota(jnp.int32, (L, L), 0) >= lax.broadcasted_iota(jnp.int32, (L, L), 1)
    scores = jnp.where(before, scores, -1e30)
    weights = jnp.exp(scores - jnp.max(scores, axis=1, keepdims=True))
    weights = (weights / jnp.sum(weights, axis=1, keepdims=True)).astype(BF16)
    out[...] = dot_nt(weights, values).astype(BF16)

    def drain(k, c):
        for g in range(NG):
            rs_copy(g, k, first.at[g]).wait_send()
            ag_copy(g, k, me).wait_send()
        return c

    lax.fori_loop(0, T - 1, drain, 0)
    for g in range(NG):
        shift_copy(g).wait_send()
    each_peer(lambda peer: gain_copy(peer, me).wait_send())
    each_peer(lambda peer: kv_copy(peer, me).wait_send())


def on_device(context, out_weight, residual, gain, q_weight, kv_weight):
    T = lax.axis_size("tensor")
    S = lax.axis_size("section")
    _, L, HD = context.shape
    B = residual.shape[2]
    D = out_weight.shape[2]
    KC = kv_weight.shape[2]
    tables = rope_tables(L, HD)
    vmem = pl.BlockSpec(memory_space=pltpu.VMEM)
    anywhere = pl.BlockSpec(memory_space=pl.ANY)
    dma = pltpu.SemaphoreType.DMA
    attended = pl.pallas_call(
        functools.partial(kernel, T, S),
        out_shape=jax.ShapeDtypeStruct((L, HD), BF16),
        in_specs=[vmem] * 7 + [anywhere] * 3,
        out_specs=vmem,
        scratch_shapes=[
            pltpu.VMEM((HD, D), BF16),
            pltpu.VMEM((D, KC), BF16),
            pltpu.VMEM((D, 2 * HD), BF16),
            pltpu.VMEM((NG, L // NG, B), BF16),
            pltpu.VMEM((NG, T - 1, L // NG, B), BF16),
            pltpu.VMEM((L, B), BF16),
            pltpu.VMEM((T, L, B), BF16),
            pltpu.VMEM((T, 1, B), F32),
            pltpu.VMEM((L, 2 * HD), F32),
            pltpu.VMEM((L, HD), F32),
            pltpu.VMEM((T, KC, L), BF16),
            dma((3,)),
            dma((NG, T - 1)), dma((NG, T - 1)),
            dma((NG,)), dma((NG,)),
            dma((NG, T - 1)), dma((NG, T - 1)),
            dma((T,)), dma((T,)),
            dma((T,)), dma((T,)),
        ],
        compiler_params=pltpu.CompilerParams(
            collective_id=0, has_side_effects=True, vmem_limit_bytes=44 * 2**20
        ),
        cost_estimate=pl.CostEstimate(
            flops=2 * L * D * HD * 3, bytes_accessed=D * HD * 6, transcendentals=L * L
        ),
        name="handover_attention",
    )(
        context[0], residual[0], gain, *[jnp.asarray(t) for t in tables],
        out_weight[0], q_weight[0], kv_weight[0],
    )
    return attended[None]


def solution(mesh):
    placed = (
        P("section", None, "tensor"),
        P("section", "tensor", None),
        P("section", None, "tensor"),
        P("section", "tensor"),
        P("section", None, "tensor"),
        P("section", None, "tensor"),
    )
    return jax.shard_map(
        on_device,
        mesh=mesh,
        in_specs=placed,
        out_specs=P("section", None, "tensor"),
        check_vma=False,
    )
```

```python
import functools

import jax
import jax.numpy as jnp
import numpy as np
from jax import lax
from jax.experimental import pallas as pl
from jax.experimental.pallas import tpu as pltpu
from jax.sharding import PartitionSpec as P

GROUP = 8
THETA = 500000.0
EPS = 1e-05
MESH = pl.DeviceIdType.MESH
BF16 = jnp.bfloat16
F32 = jnp.float32
NG = 4
SKEW = 2


def rope_tables(length, head_size):
    half = head_size // 2
    frequency = np.float32(THETA) ** (-(np.arange(half, dtype=np.float32) * np.float32(2.0) / np.float32(head_size)))
    angles = np.arange(length, dtype=np.float32)[:, None] * frequency.astype(np.float32)[None, :]
    cosine, sine = np.cos(angles).astype(np.float32), np.sin(angles).astype(np.float32)
    return (
        np.concatenate([cosine, cosine], axis=1),
        np.concatenate([-sine, sine], axis=1),
        np.ascontiguousarray(np.concatenate([cosine, cosine], axis=1).T),
        np.ascontiguousarray(np.concatenate([-sine, sine], axis=1).T),
    )


def dot_nt(a, b):
    return lax.dot_general(a, b, (((1,), (1,)), ((), ())), preferred_element_type=F32)


def kernel(
    T, S,
    ctx, res, gain, cos_q, sin_q, cos_k, sin_k, ow_hbm, qw_hbm, kvw_hbm,
    out,
    ow, kvw, w, first, rs, hand, xb, gains, acc, ssq, kvall, keys, values,
    ow_sem, load_sem, rs_send, rs_recv, sh_send, sh_recv, ag_send, ag_recv, g_send, g_recv, kv_send, kv_recv,
):
    L, HD = ctx.shape
    B = res.shape[1]
    D = ow.shape[1]
    KC = kvw.shape[0]
    R = L // 4
    half = L // 2
    sec = lax.axis_index("section")
    me = lax.axis_index("tensor")

    def ring(pos):
        upper = pos // (T // 2)
        return (1 - upper) * (2 * pos) + upper * (2 * (T - 1 - pos) + 1)

    y = me % 2
    p = (1 - y) * (me // 2) + y * (T - 1 - me // 2)

    def at(offset):
        return ring((p + offset + 2 * T) % T)

    sides = (at(1), at(-1))
    signs = (1, -1)
    following = (sec + 1) % S
    previous = (sec + S - 1) % S

    def block(owner):
        return pl.ds(pl.multiple_of(owner * B, B), B)

    def ow_copy(owner):
        return pltpu.make_async_copy(ow_hbm.at[:, block(owner)], ow.at[:, block(owner)], ow_sem.at[owner])

    for side in range(2):
        ow_copy(sides[side]).start()

    def load_rest(j, c):
        ow_copy(at(j)).start()
        return c

    def wait_rest(j, c):
        ow_copy(at(j)).wait()
        return c

    lax.fori_loop(2, T - 1, load_rest, 0)
    ow_copy(me).start()
    kv_load = pltpu.make_async_copy(kvw_hbm, kvw, load_sem.at[0])
    kv_load.start()
    q_load = pltpu.make_async_copy(qw_hbm, w.at[:, pl.ds(0, HD)], load_sem.at[1])
    q_load.start()

    barrier = pltpu.get_barrier_semaphore()

    def each_peer(act):
        def step(j, c):
            act((me + j) % T)
            return c

        lax.fori_loop(1, T, step, 0)

    def greet(s, t):
        pl.semaphore_signal(barrier, inc=1, device_id=(s, t), device_id_type=MESH)

    each_peer(lambda peer: greet(sec, peer))
    greet(following, me)
    greet(previous, me)

    def rows(c, side):
        return pl.ds(c * half + side * R, R)

    def rs_copy(c, side, k, source):
        g = 2 * c + side
        return pltpu.make_async_remote_copy(
            src_ref=source, dst_ref=rs.at[g, k], send_sem=rs_send.at[g, k], recv_sem=rs_recv.at[g, k],
            device_id=(sec, sides[side]), device_id_type=MESH,
        )

    def shift_copy(c, side):
        g = 2 * c + side
        return pltpu.make_async_remote_copy(
            src_ref=hand.at[rows(c, side)], dst_ref=xb.at[me, rows(c, side)],
            send_sem=sh_send.at[g], recv_sem=sh_recv.at[g],
            device_id=(following, me), device_id_type=MESH,
        )

    def ag_copy(c, side, k, owner):
        g = 2 * c + side
        return pltpu.make_async_remote_copy(
            src_ref=xb.at[owner, rows(c, side)], dst_ref=xb.at[owner, rows(c, side)],
            send_sem=ag_send.at[g, k], recv_sem=ag_recv.at[g, k],
            device_id=(sec, sides[side]), device_id_type=MESH,
        )

    def gain_copy(peer, slot):
        return pltpu.make_async_remote_copy(
            src_ref=gain, dst_ref=gains.at[slot], send_sem=g_send.at[peer], recv_sem=g_recv.at[slot],
            device_id=(sec, peer), device_id_type=MESH,
        )

    def kv_copy(c, peer, slot):
        columns = pl.ds(c * half, half)
        return pltpu.make_async_remote_copy(
            src_ref=kvall.at[me, :, columns], dst_ref=kvall.at[slot, :, columns],
            send_sem=kv_send.at[c, peer], recv_sem=kv_recv.at[c, slot],
            device_id=(sec, peer), device_id_type=MESH,
        )

    def term(c, side, owner):
        return jnp.dot(ctx[rows(c, side), :], ow[:, block(owner)], preferred_element_type=F32)

    def start_terms(c):
        for side in range(2):
            first[2 * c + side] = term(c, side, at(-signs[side])).astype(BF16)

    def start_sends(c):
        for side in range(2):
            rs_copy(c, side, 0, first.at[2 * c + side]).start()

    def reduce(c, k):
        parts = [term(c, side, at(-signs[side] * (2 + k))) for side in range(2)]
        for side in range(2):
            g = 2 * c + side
            rs_copy(c, side, k, first.at[g]).wait_recv()
            rs[g, k] = (rs[g, k].astype(F32) + parts[side]).astype(BF16)
            rs_copy(c, side, k + 1, rs.at[g, k]).start()

    def hand_over(c):
        parts = [term(c, side, me) + res[rows(c, side), :].astype(F32) for side in range(2)]
        for side in range(2):
            g = 2 * c + side
            rs_copy(c, side, T - 2, first.at[g]).wait_recv()
            hand[rows(c, side), :] = (rs[g, T - 2].astype(F32) + parts[side]).astype(BF16)
            shift_copy(c, side).start()

    def project(c, side, owner):
        features = xb[owner, rows(c, side), :].astype(F32)
        scaled = (features * gains[owner]).astype(BF16)
        squares = features * features
        total = squares[:, :HD]
        for i in range(1, B // HD):
            total = total + squares[:, i * HD:(i + 1) * HD]
        ssq[rows(c, side), :] += total
        acc[rows(c, side), :] += jnp.dot(scaled, w[block(owner), :], preferred_element_type=F32)

    def spread(c):
        for side in range(2):
            shift_copy(c, side).wait_recv()
            ag_copy(c, side, 0, me).start()
        for side in range(2):
            project(c, side, me)

    def pass_on(c, k):
        owners = [at(-signs[side] * (1 + k)) for side in range(2)]
        for side in range(2):
            ag_copy(c, side, k, owners[side]).wait_recv()
            ag_copy(c, side, k + 1, owners[side]).start()
        for side in range(2):
            project(c, side, owners[side])

    def arrive(c):
        owners = [at(-signs[side] * (T - 1)) for side in range(2)]
        for side in range(2):
            ag_copy(c, side, T - 2, owners[side]).wait_recv()
            project(c, side, owners[side])

    def place(i):
        w[block(i), HD:] = jnp.concatenate(
            [jnp.transpose(kvw[:, block(i)]), jnp.zeros((B, HD - KC), BF16)], axis=1
        )

    for side in range(2):
        ow_copy(sides[side]).wait()
    start_terms(0)
    pl.semaphore_wait(barrier, T + 1)
    start_sends(0)

    gains[me] = gain[...]
    each_peer(lambda peer: gain_copy(peer, me).start())
    start_terms(1)
    acc[...] = jnp.zeros_like(acc)
    ssq[...] = jnp.zeros_like(ssq)
    lax.fori_loop(2, T - 1, wait_rest, 0)
    ow_copy(me).wait()
    kv_load.wait()
    place(T - 2)
    place(T - 1)
    each_peer(lambda peer: gain_copy(peer, peer).wait_recv())
    q_load.wait()

    def slot(j, c):
        for cls in range(2):
            i = j - SKEW * cls
            if cls:
                pl.when(i == -1)(lambda: start_sends(1))
            pl.when((i >= 0) & (i < T - 2))(functools.partial(reduce, cls, i))
            pl.when(i == T - 2)(functools.partial(hand_over, cls))
            pl.when(i == T - 1)(functools.partial(spread, cls))
            pl.when((i >= T) & (i < 2 * T - 2))(functools.partial(pass_on, cls, i - T))
        pl.when(j < T - 2)(functools.partial(place, j))
        return c

    lax.fori_loop(0, 2 * T - 2, slot, 0)

    share = HD // T
    shift = share.bit_length() - 1
    feature = lax.broadcasted_iota(jnp.int32, (HD, T * KC), 0)
    column = lax.broadcasted_iota(jnp.int32, (HD, T * KC), 1)
    source = (feature >> shift) * KC + (feature & (share - 1)) + (me // GROUP) * (2 * share)
    key_picks = (column == source).astype(F32).astype(BF16)
    value_picks = (column == source + share).astype(F32).astype(BF16)
    eye = lax.broadcasted_iota(jnp.int32, (KC, HD), 0) == lax.broadcasted_iota(jnp.int32, (KC, HD), 1)
    eye = eye.astype(F32).astype(BF16)

    def finish(c):
        part = pl.ds(c * half, half)
        factor = lax.rsqrt(jnp.sum(ssq[part, :], axis=1, keepdims=True) * (1.0 / D) + EPS)
        pairs = (acc[part, HD:] * factor).astype(BF16)
        kvall[me, :, part] = dot_nt(eye, pairs).astype(BF16)
        each_peer(lambda peer: kv_copy(c, peer, me).start())
        queries = acc[part, :HD] * factor
        turned = jnp.concatenate([queries[:, HD // 2:], queries[:, :HD // 2]], axis=1)
        return (queries * cos_q[part, :] + turned * sin_q[part, :]).astype(BF16)

    def attend(c, queries):
        part = pl.ds(c * half, half)
        each_peer(lambda peer: kv_copy(c, peer, peer).wait_recv())
        everything = kvall[:, :, part].reshape(T * KC, half)
        found = jnp.dot(key_picks, everything, preferred_element_type=F32)
        turned = jnp.concatenate([found[HD // 2:], found[:HD // 2]], axis=0)
        keys[:, part] = (found * cos_k[:, part] + turned * sin_k[:, part]).astype(BF16)
        values[:, part] = jnp.dot(value_picks, everything, preferred_element_type=F32).astype(BF16)
        seen = (c + 1) * half
        scores = jnp.dot(queries, keys[:, :seen], preferred_element_type=F32) * (HD ** -0.5)
        before = lax.broadcasted_iota(jnp.int32, (half, seen), 0) + c * half >= lax.broadcasted_iota(
            jnp.int32, (half, seen), 1
        )
        scores = jnp.where(before, scores, -1e30)
        weights = jnp.exp(scores - jnp.max(scores, axis=1, keepdims=True))
        weights = (weights / jnp.sum(weights, axis=1, keepdims=True)).astype(BF16)
        out[part, :] = dot_nt(weights, values[:, :seen]).astype(BF16)

    arrive(0)
    pass_on(1, T - 2 - SKEW)
    queries = finish(0)

    def late(k, c):
        pass_on(1, k)
        return c

    lax.fori_loop(T - 1 - SKEW, T - 2, late, 0)
    attend(0, queries)
    arrive(1)
    attend(1, finish(1))

    def drain(k, c):
        for cls in range(2):
            for side in range(2):
                rs_copy(cls, side, k, first.at[0]).wait_send()
                ag_copy(cls, side, k, me).wait_send()
        return c

    lax.fori_loop(0, T - 1, drain, 0)
    for cls in range(2):
        for side in range(2):
            shift_copy(cls, side).wait_send()
        each_peer(lambda peer: kv_copy(cls, peer, me).wait_send())
    each_peer(lambda peer: gain_copy(peer, me).wait_send())


def on_device(context, out_weight, residual, gain, q_weight, kv_weight):
    T = lax.axis_size("tensor")
    S = lax.axis_size("section")
    _, L, HD = context.shape
    B = residual.shape[2]
    D = out_weight.shape[2]
    KC = kv_weight.shape[2]
    tables = rope_tables(L, HD)
    vmem = pl.BlockSpec(memory_space=pltpu.VMEM)
    anywhere = pl.BlockSpec(memory_space=pl.ANY)
    dma = pltpu.SemaphoreType.DMA
    attended = pl.pallas_call(
        functools.partial(kernel, T, S),
        out_shape=jax.ShapeDtypeStruct((L, HD), BF16),
        in_specs=[vmem] * 7 + [anywhere] * 3,
        out_specs=vmem,
        scratch_shapes=[
            pltpu.VMEM((HD, D), BF16),
            pltpu.VMEM((KC, D), BF16),
            pltpu.VMEM((D, 2 * HD), BF16),
            pltpu.VMEM((NG, L // NG, B), BF16),
            pltpu.VMEM((NG, T - 1, L // NG, B), BF16),
            pltpu.VMEM((L, B), BF16),
            pltpu.VMEM((T, L, B), BF16),
            pltpu.VMEM((T, 1, B), F32),
            pltpu.VMEM((L, 2 * HD), F32),
            pltpu.VMEM((L, HD), F32),
            pltpu.VMEM((T, KC, L), BF16),
            pltpu.VMEM((HD, L), BF16),
            pltpu.VMEM((HD, L), BF16),
            dma((T,)), dma((2,)),
            dma((NG, T - 1)), dma((NG, T - 1)),
            dma((NG,)), dma((NG,)),
            dma((NG, T - 1)), dma((NG, T - 1)),
            dma((T,)), dma((T,)),
            dma((2, T)), dma((2, T)),
        ],
        compiler_params=pltpu.CompilerParams(
            collective_id=0, has_side_effects=True, vmem_limit_bytes=62 * 2**20
        ),
        cost_estimate=pl.CostEstimate(
            flops=2 * L * D * HD * 3, bytes_accessed=D * HD * 6, transcendentals=L * L
        ),
        name="handover_attention",
    )(
        context[0], residual[0], gain, *[jnp.asarray(t) for t in tables],
        out_weight[0], q_weight[0], jnp.swapaxes(kv_weight[0], 0, 1),
    )
    return attended[None]


def solution(mesh):
    placed = (
        P("section", None, "tensor"),
        P("section", "tensor", None),
        P("section", None, "tensor"),
        P("section", "tensor"),
        P("section", None, "tensor"),
        P("section", None, "tensor"),
    )
    return jax.shard_map(
        on_device,
        mesh=mesh,
        in_specs=placed,
        out_specs=P("section", None, "tensor"),
        check_vma=False,
    )
```

```python
import functools

import jax
import jax.numpy as jnp
import numpy as np
from jax import lax
from jax.experimental import pallas as pl
from jax.experimental.pallas import tpu as pltpu
from jax.sharding import PartitionSpec as P

GROUP = 8
THETA = 500000.0
EPS = 1e-05
MESH = pl.DeviceIdType.MESH
BF16 = jnp.bfloat16
F32 = jnp.float32
NG = 8


def rope_tables(length, head_size):
    half = head_size // 2
    frequency = np.float32(THETA) ** (-(np.arange(half, dtype=np.float32) * np.float32(2.0) / np.float32(head_size)))
    angles = np.arange(length, dtype=np.float32)[:, None] * frequency.astype(np.float32)[None, :]
    cosine, sine = np.cos(angles).astype(np.float32), np.sin(angles).astype(np.float32)
    return (
        np.concatenate([cosine, cosine], axis=1),
        np.concatenate([-sine, sine], axis=1),
        np.ascontiguousarray(np.concatenate([cosine, cosine], axis=1).T),
        np.ascontiguousarray(np.concatenate([-sine, sine], axis=1).T),
    )


def dot_nt(a, b):
    return lax.dot_general(a, b, (((1,), (1,)), ((), ())), preferred_element_type=F32)


def kernel(
    T, S,
    ctx, res, gain, cos_q, sin_q, cos_k, sin_k, ow_hbm, qw_hbm, kvw_hbm,
    out,
    ow, kvw, w, first, rs, hand, xb, gains, acc, ssq, kvall, terms,
    ow_sem, load_sem, rs_send, rs_recv, sh_send, sh_recv, ag_send, ag_recv, g_send, g_recv, kv_send, kv_recv,
):
    L, HD = ctx.shape
    B = res.shape[1]
    D = ow.shape[1]
    KC = kvw.shape[0]
    R = L // NG
    per_side = NG // 2
    half = L // 2
    sec = lax.axis_index("section")
    me = lax.axis_index("tensor")

    def ring(pos):
        upper = pos // (T // 2)
        return (1 - upper) * (2 * pos) + upper * (2 * (T - 1 - pos) + 1)

    y = me % 2
    p = (1 - y) * (me // 2) + y * (T - 1 - me // 2)

    def at(offset):
        return ring((p + offset + 2 * T) % T)

    sides = (at(1), at(-1))
    signs = (1, -1)
    following = (sec + 1) % S
    previous = (sec + S - 1) % S

    def block(owner):
        return pl.ds(pl.multiple_of(owner * B, B), B)

    def ow_copy(owner):
        return pltpu.make_async_copy(ow_hbm.at[:, block(owner)], ow.at[:, block(owner)], ow_sem.at[owner])

    for side in range(2):
        ow_copy(sides[side]).start()

    def load_rest(j, c):
        ow_copy(at(j)).start()
        return c

    def wait_rest(j, c):
        ow_copy(at(j)).wait()
        return c

    lax.fori_loop(2, T - 1, load_rest, 0)
    ow_copy(me).start()
    kv_load = pltpu.make_async_copy(kvw_hbm, kvw, load_sem.at[0])
    kv_load.start()
    q_load = pltpu.make_async_copy(qw_hbm, w.at[:, pl.ds(0, HD)], load_sem.at[1])
    q_load.start()

    barrier = pltpu.get_barrier_semaphore()

    def each_peer(act):
        def step(j, c):
            act((me + j) % T)
            return c

        lax.fori_loop(1, T, step, 0)

    def greet(s, t):
        pl.semaphore_signal(barrier, inc=1, device_id=(s, t), device_id_type=MESH)

    each_peer(lambda peer: greet(sec, peer))
    greet(following, me)
    greet(previous, me)

    def rows(g):
        return pl.ds(g * R, R)

    def side_of(g):
        return g // per_side

    order = [side * per_side + j for j in range(per_side) for side in range(2)]

    def rs_copy(g, k, source):
        return pltpu.make_async_remote_copy(
            src_ref=source, dst_ref=rs.at[g, k], send_sem=rs_send.at[g, k], recv_sem=rs_recv.at[g, k],
            device_id=(sec, sides[side_of(g)]), device_id_type=MESH,
        )

    def shift_copy(g):
        return pltpu.make_async_remote_copy(
            src_ref=hand.at[rows(g)], dst_ref=xb.at[me, rows(g)], send_sem=sh_send.at[g], recv_sem=sh_recv.at[g],
            device_id=(following, me), device_id_type=MESH,
        )

    def ag_copy(g, k, owner):
        return pltpu.make_async_remote_copy(
            src_ref=xb.at[owner, rows(g)], dst_ref=xb.at[owner, rows(g)],
            send_sem=ag_send.at[g, k], recv_sem=ag_recv.at[g, k],
            device_id=(sec, sides[side_of(g)]), device_id_type=MESH,
        )

    def gain_copy(peer, slot):
        return pltpu.make_async_remote_copy(
            src_ref=gain, dst_ref=gains.at[slot], send_sem=g_send.at[peer], recv_sem=g_recv.at[slot],
            device_id=(sec, peer), device_id_type=MESH,
        )

    def kv_copy(peer, slot):
        return pltpu.make_async_remote_copy(
            src_ref=kvall.at[me], dst_ref=kvall.at[slot], send_sem=kv_send.at[peer], recv_sem=kv_recv.at[slot],
            device_id=(sec, peer), device_id_type=MESH,
        )

    def half_rows(side):
        return pl.ds(side * half, half)

    def set_terms(side, owner):
        terms[half_rows(side), :] = jnp.dot(
            ctx[half_rows(side), :], ow[:, block(owner)], preferred_element_type=F32
        )

    def project(side, owner):
        features = xb[owner, half_rows(side), :].astype(F32)
        scaled = (features * gains[owner]).astype(BF16)
        squares = features * features
        total = squares[:, :HD]
        for i in range(1, B // HD):
            total = total + squares[:, i * HD:(i + 1) * HD]
        ssq[half_rows(side), :] += total
        acc[half_rows(side), :] += jnp.dot(scaled, w[block(owner), :], preferred_element_type=F32)

    def place(i):
        w[block(i), HD:] = jnp.concatenate(
            [jnp.transpose(kvw[:, block(i)]), jnp.zeros((B, HD - KC), BF16)], axis=1
        )

    for side in range(2):
        ow_copy(sides[1 - side]).wait()
        first[half_rows(side), :] = jnp.dot(
            ctx[half_rows(side), :], ow[:, block(sides[1 - side])], preferred_element_type=F32
        ).astype(BF16)
    pl.semaphore_wait(barrier, T + 1)
    for g in order:
        rs_copy(g, 0, first.at[rows(g)]).start()

    lax.fori_loop(2, T - 1, wait_rest, 0)
    ow_copy(me).wait()
    for side in range(2):
        set_terms(side, at(-2 * signs[side]))
    gains[me] = gain[...]
    each_peer(lambda peer: gain_copy(peer, me).start())
    acc[...] = jnp.zeros_like(acc)
    ssq[...] = jnp.zeros_like(ssq)
    kv_load.wait()
    place(T - 2)
    place(T - 1)

    def reduce_step(k, c):
        for g in order:
            rs_copy(g, k, first.at[rows(g)]).wait_recv()
            rs[g, k] = (rs[g, k].astype(F32) + terms[rows(g), :]).astype(BF16)
            rs_copy(g, k + 1, rs.at[g, k]).start()
        for side in range(2):
            set_terms(side, at(-signs[side] * (3 + k)))
        place(k)
        return c

    lax.fori_loop(0, T - 2, reduce_step, 0)

    for g in order:
        rs_copy(g, T - 2, first.at[rows(g)]).wait_recv()
        total = rs[g, T - 2].astype(F32) + terms[rows(g), :]
        hand[rows(g), :] = (res[rows(g), :].astype(F32) + total).astype(BF16)
        shift_copy(g).start()

    each_peer(lambda peer: gain_copy(peer, peer).wait_recv())
    q_load.wait()
    for g in order:
        shift_copy(g).wait_recv()
        ag_copy(g, 0, me).start()
    for side in range(2):
        project(side, me)

    def gather_step(k, c):
        owners = [at(-signs[side] * (1 + k)) for side in range(2)]
        for g in order:
            ag_copy(g, k, owners[side_of(g)]).wait_recv()
            ag_copy(g, k + 1, owners[side_of(g)]).start()
        for side in range(2):
            project(side, owners[side])
        return c

    lax.fori_loop(0, T - 2, gather_step, 0)
    for g in order:
        ag_copy(g, T - 2, at(-signs[side_of(g)] * (T - 1))).wait_recv()
    for side in range(2):
        project(side, at(-signs[side] * (T - 1)))

    factor = lax.rsqrt(jnp.sum(ssq[...], axis=1, keepdims=True) * (1.0 / D) + EPS)
    pairs = (acc[:, HD:] * factor).astype(BF16)
    eye = lax.broadcasted_iota(jnp.int32, (KC, HD), 0) == lax.broadcasted_iota(jnp.int32, (KC, HD), 1)
    kvall[me] = dot_nt(eye.astype(F32).astype(BF16), pairs).astype(BF16)
    each_peer(lambda peer: kv_copy(peer, me).start())

    queries = acc[:, :HD] * factor
    turned = jnp.concatenate([queries[:, HD // 2:], queries[:, :HD // 2]], axis=1)
    queries = (queries * cos_q[...] + turned * sin_q[...]).astype(BF16)

    share = HD // T
    shift = share.bit_length() - 1
    feature = lax.broadcasted_iota(jnp.int32, (HD, T * KC), 0)
    column = lax.broadcasted_iota(jnp.int32, (HD, T * KC), 1)
    source = (feature >> shift) * KC + (feature & (share - 1)) + (me // GROUP) * (2 * share)
    key_picks = (column == source).astype(F32).astype(BF16)
    value_picks = (column == source + share).astype(F32).astype(BF16)

    each_peer(lambda peer: kv_copy(peer, peer).wait_recv())
    everything = kvall[...].reshape(T * KC, L)
    keys = jnp.dot(key_picks, everything, preferred_element_type=F32)
    values = jnp.dot(value_picks, everything, preferred_element_type=F32).astype(BF16)
    turned = jnp.concatenate([keys[HD // 2:], keys[:HD // 2]], axis=0)
    keys = (keys * cos_k[...] + turned * sin_k[...]).astype(BF16)
    for c in range(2):
        seen = (c + 1) * half
        scores = jnp.dot(queries[c * half:seen], keys[:, :seen], preferred_element_type=F32) * (HD ** -0.5)
        before = lax.broadcasted_iota(jnp.int32, (half, seen), 0) + c * half >= lax.broadcasted_iota(
            jnp.int32, (half, seen), 1
        )
        scores = jnp.where(before, scores, -1e30)
        weights = jnp.exp(scores - jnp.max(scores, axis=1, keepdims=True))
        weights = (weights * (1.0 / jnp.sum(weights, axis=1, keepdims=True))).astype(BF16)
        out[half_rows(c), :] = dot_nt(weights, values[:, :seen]).astype(BF16)

    def drain(k, c):
        for g in range(NG):
            rs_copy(g, k, first.at[rows(g)]).wait_send()
            ag_copy(g, k, me).wait_send()
        return c

    lax.fori_loop(0, T - 1, drain, 0)
    for g in range(NG):
        shift_copy(g).wait_send()
    each_peer(lambda peer: gain_copy(peer, me).wait_send())
    each_peer(lambda peer: kv_copy(peer, me).wait_send())


def on_device(context, out_weight, residual, gain, q_weight, kv_weight):
    T = lax.axis_size("tensor")
    S = lax.axis_size("section")
    _, L, HD = context.shape
    B = residual.shape[2]
    D = out_weight.shape[2]
    KC = kv_weight.shape[2]
    tables = rope_tables(L, HD)
    vmem = pl.BlockSpec(memory_space=pltpu.VMEM)
    anywhere = pl.BlockSpec(memory_space=pl.ANY)
    dma = pltpu.SemaphoreType.DMA
    attended = pl.pallas_call(
        functools.partial(kernel, T, S),
        out_shape=jax.ShapeDtypeStruct((L, HD), BF16),
        in_specs=[vmem] * 7 + [anywhere] * 3,
        out_specs=vmem,
        scratch_shapes=[
            pltpu.VMEM((HD, D), BF16),
            pltpu.VMEM((KC, D), BF16),
            pltpu.VMEM((D, 2 * HD), BF16),
            pltpu.VMEM((L, B), BF16),
            pltpu.VMEM((NG, T - 1, L // NG, B), BF16),
            pltpu.VMEM((L, B), BF16),
            pltpu.VMEM((T, L, B), BF16),
            pltpu.VMEM((T, 1, B), F32),
            pltpu.VMEM((L, 2 * HD), F32),
            pltpu.VMEM((L, HD), F32),
            pltpu.VMEM((T, KC, L), BF16),
            pltpu.VMEM((L, B), F32),
            dma((T,)), dma((2,)),
            dma((NG, T - 1)), dma((NG, T - 1)),
            dma((NG,)), dma((NG,)),
            dma((NG, T - 1)), dma((NG, T - 1)),
            dma((T,)), dma((T,)),
            dma((T,)), dma((T,)),
        ],
        compiler_params=pltpu.CompilerParams(
            collective_id=0, has_side_effects=True, vmem_limit_bytes=62 * 2**20
        ),
        cost_estimate=pl.CostEstimate(
            flops=2 * L * D * HD * 3, bytes_accessed=D * HD * 6, transcendentals=L * L
        ),
        name="handover_attention",
    )(
        context[0], residual[0], gain, *[jnp.asarray(t) for t in tables],
        out_weight[0], q_weight[0], jnp.swapaxes(kv_weight[0], 0, 1),
    )
    return attended[None]


def solution(mesh):
    placed = (
        P("section", None, "tensor"),
        P("section", "tensor", None),
        P("section", None, "tensor"),
        P("section", "tensor"),
        P("section", None, "tensor"),
        P("section", None, "tensor"),
    )
    return jax.shard_map(
        on_device,
        mesh=mesh,
        in_specs=placed,
        out_specs=P("section", None, "tensor"),
        check_vma=False,
    )
```

```python
import functools

import jax
import jax.numpy as jnp
import numpy as np
from jax import lax
from jax.experimental import pallas as pl
from jax.experimental.pallas import tpu as pltpu
from jax.sharding import PartitionSpec as P

GROUP = 8
THETA = 500000.0
EPS = 1e-05
MESH = pl.DeviceIdType.MESH
BF16 = jnp.bfloat16
F32 = jnp.float32
NG = 4


def rope_tables(length, head_size):
    half = head_size // 2
    frequency = np.float32(THETA) ** (-(np.arange(half, dtype=np.float32) * np.float32(2.0) / np.float32(head_size)))
    angles = np.arange(length, dtype=np.float32)[:, None] * frequency.astype(np.float32)[None, :]
    cosine, sine = np.cos(angles).astype(np.float32), np.sin(angles).astype(np.float32)
    return (
        np.concatenate([cosine, cosine], axis=1),
        np.concatenate([-sine, sine], axis=1),
        np.ascontiguousarray(np.concatenate([cosine, cosine], axis=1).T),
        np.ascontiguousarray(np.concatenate([-sine, sine], axis=1).T),
    )


def dot_nt(a, b):
    return lax.dot_general(a, b, (((1,), (1,)), ((), ())), preferred_element_type=F32)


def kernel(
    T, S,
    ctx, res, gain, cos_q, sin_q, cos_k, sin_k, ow_hbm, qw_hbm, kvw_hbm,
    out,
    ow, kvw, w, first, rs, hand, xb, gains, acc, ssq, kvall, terms,
    ow_sem, load_sem, rs_send, rs_recv, sh_send, sh_recv, ag_send, ag_recv, g_send, g_recv, kv_send, kv_recv,
):
    L, HD = ctx.shape
    B = res.shape[1]
    D = ow.shape[1]
    KC = kvw.shape[0]
    R = L // NG
    H = T // 2
    half = L // 2
    sec = lax.axis_index("section")
    me = lax.axis_index("tensor")

    def ring(pos):
        upper = pos // (T // 2)
        return (1 - upper) * (2 * pos) + upper * (2 * (T - 1 - pos) + 1)

    y = me % 2
    p = (1 - y) * (me // 2) + y * (T - 1 - me // 2)

    def at(offset):
        return ring((p + offset + 2 * T) % T)

    sides = (at(1), at(-1))
    signs = (1, -1)
    following = (sec + 1) % S
    previous = (sec + S - 1) % S

    def block(owner):
        return pl.ds(pl.multiple_of(owner * B, B), B)

    def ow_copy(owner):
        return pltpu.make_async_copy(ow_hbm.at[:, block(owner)], ow.at[:, block(owner)], ow_sem.at[owner])

    ow_copy(at(H)).start()
    ow_copy(at(H - 1)).start()
    ow_copy(at(1 - H)).start()

    def load_rest(j, c):
        ow_copy(at(j)).start()
        return c

    def wait_rest(j, c):
        ow_copy(at(j)).wait()
        return c

    lax.fori_loop(T + 2 - H, T + H - 1, load_rest, 0)
    kv_load = pltpu.make_async_copy(kvw_hbm, kvw, load_sem.at[0])
    kv_load.start()
    q_load = pltpu.make_async_copy(qw_hbm, w.at[:, pl.ds(0, HD)], load_sem.at[1])
    q_load.start()

    barrier = pltpu.get_barrier_semaphore()

    def each_peer(act):
        def step(j, c):
            act((me + j) % T)
            return c

        lax.fori_loop(1, T, step, 0)

    def greet(s, t):
        pl.semaphore_signal(barrier, inc=1, device_id=(s, t), device_id_type=MESH)

    each_peer(lambda peer: greet(sec, peer))
    greet(following, me)
    greet(previous, me)

    def rows(g):
        return pl.ds(g * R, R)

    def is_long(side, g):
        return (g // (NG // 2)) == side

    order = [g for j in range(NG // 2) for g in (j, j + NG // 2)]
    pairs_of = [(side, g) for g in order for side in range(2)]

    def rs_copy(side, g, left, source):
        return pltpu.make_async_remote_copy(
            src_ref=source, dst_ref=rs.at[side, left - 1, rows(g)],
            send_sem=rs_send.at[side, g, left - 1], recv_sem=rs_recv.at[side, g, left - 1],
            device_id=(sec, sides[side]), device_id_type=MESH,
        )

    def shift_copy(g):
        return pltpu.make_async_remote_copy(
            src_ref=hand.at[rows(g)], dst_ref=xb.at[me, rows(g)], send_sem=sh_send.at[g], recv_sem=sh_recv.at[g],
            device_id=(following, me), device_id_type=MESH,
        )

    def ag_copy(side, g, k, owner):
        return pltpu.make_async_remote_copy(
            src_ref=xb.at[owner, rows(g)], dst_ref=xb.at[owner, rows(g)],
            send_sem=ag_send.at[side, g, k], recv_sem=ag_recv.at[side, g, k],
            device_id=(sec, sides[side]), device_id_type=MESH,
        )

    def gain_copy(peer, slot):
        return pltpu.make_async_remote_copy(
            src_ref=gain, dst_ref=gains.at[slot], send_sem=g_send.at[peer], recv_sem=g_recv.at[slot],
            device_id=(sec, peer), device_id_type=MESH,
        )

    def kv_copy(peer, slot):
        return pltpu.make_async_remote_copy(
            src_ref=kvall.at[me], dst_ref=kvall.at[slot], send_sem=kv_send.at[peer], recv_sem=kv_recv.at[slot],
            device_id=(sec, peer), device_id_type=MESH,
        )

    def half_rows(side):
        return pl.ds(side * half, half)

    def term(owner):
        return jnp.dot(ctx[...], ow[:, block(owner)], preferred_element_type=F32)

    def project(owner):
        features = xb[owner].astype(F32)
        scaled = (features * gains[owner]).astype(BF16)
        squares = features * features
        total = squares[:, :HD]
        for i in range(1, B // HD):
            total = total + squares[:, i * HD:(i + 1) * HD]
        ssq[...] += total
        acc[...] += jnp.dot(scaled, w[block(owner), :], preferred_element_type=F32)

    def place(i):
        w[block(i), HD:] = jnp.concatenate(
            [jnp.transpose(kvw[:, block(i)]), jnp.zeros((B, HD - KC), BF16)], axis=1
        )

    ow_copy(at(H)).wait()
    first[...] = term(at(H)).astype(BF16)
    pl.semaphore_wait(barrier, T + 1)
    for side, g in pairs_of:
        if is_long(side, g):
            rs_copy(side, g, H, first.at[rows(g)]).start()

    for side in range(2):
        ow_copy(at(signs[side] * (H - 1))).wait()
        terms[side] = term(at(signs[side] * (H - 1)))
    for side, g in pairs_of:
        if not is_long(side, g):
            rs[side, H - 1, rows(g), :] = terms[side, rows(g), :].astype(BF16)
            rs_copy(side, g, H - 1, rs.at[side, H - 1, rows(g)]).start()
    gains[me] = gain[...]
    each_peer(lambda peer: gain_copy(peer, me).start())

    for side, g in pairs_of:
        if is_long(side, g):
            rs_copy(side, g, H, first.at[rows(g)]).wait_recv()
            total = rs[side, H - 1, rows(g), :].astype(F32) + terms[side, rows(g), :]
            rs[side, H - 1, rows(g), :] = total.astype(BF16)
            rs_copy(side, g, H - 1, rs.at[side, H - 1, rows(g)]).start()

    lax.fori_loop(T + 2 - H, T + H - 1, wait_rest, 0)
    for side in range(2):
        terms[side] = term(at(signs[side] * (H - 2)))
    acc[...] = jnp.zeros_like(acc)
    ssq[...] = jnp.zeros_like(ssq)
    kv_load.wait()
    place(T - 2)
    place(T - 1)

    def reduce_step(i, c):
        left = H - 2 - i
        for side, g in pairs_of:
            rs_copy(side, g, left + 1, first.at[rows(g)]).wait_recv()
            total = rs[side, left, rows(g), :].astype(F32) + terms[side, rows(g), :]
            rs[side, left, rows(g), :] = total.astype(BF16)
            rs_copy(side, g, left, rs.at[side, left, rows(g)]).start()
        for side in range(2):
            terms[side] = term(at(signs[side] * (left - 1)))
        for n in range(2):
            place(2 * i + n)
        return c

    lax.fori_loop(0, H - 2, reduce_step, 0)
    terms[0] += res[...].astype(F32)
    for g in order:
        for side in range(2):
            rs_copy(side, g, 1, first.at[rows(g)]).wait_recv()
        total = rs[0, 0, rows(g), :].astype(F32) + rs[1, 0, rows(g), :].astype(F32) + terms[0, rows(g), :]
        hand[rows(g), :] = total.astype(BF16)
        shift_copy(g).start()
    place(T - 4)
    place(T - 3)

    each_peer(lambda peer: gain_copy(peer, peer).wait_recv())
    q_load.wait()
    for g in order:
        shift_copy(g).wait_recv()
        for side in range(2):
            ag_copy(side, g, 0, me).start()
    project(me)

    def gather_step(k, c):
        owners = [at(-signs[side] * (1 + k)) for side in range(2)]
        for side, g in pairs_of:
            ag_copy(side, g, k, owners[side]).wait_recv()
            ag_copy(side, g, k + 1, owners[side]).start()
        for side in range(2):
            project(owners[side])
        return c

    lax.fori_loop(0, H - 2, gather_step, 0)
    owners = [at(-signs[side] * (H - 1)) for side in range(2)]
    for wanted in (True, False):
        for side, g in pairs_of:
            if is_long(side, g) == wanted:
                ag_copy(side, g, H - 2, owners[side]).wait_recv()
                if wanted:
                    ag_copy(side, g, H - 1, owners[side]).start()
    for side in range(2):
        project(owners[side])
    for side, g in pairs_of:
        if is_long(side, g):
            ag_copy(side, g, H - 1, at(H)).wait_recv()
    project(at(H))

    factor = lax.rsqrt(jnp.sum(ssq[...], axis=1, keepdims=True) * (1.0 / D) + EPS)
    pairs = (acc[:, HD:] * factor).astype(BF16)
    eye = lax.broadcasted_iota(jnp.int32, (KC, HD), 0) == lax.broadcasted_iota(jnp.int32, (KC, HD), 1)
    kvall[me] = dot_nt(eye.astype(F32).astype(BF16), pairs).astype(BF16)
    each_peer(lambda peer: kv_copy(peer, me).start())

    queries = acc[:, :HD] * factor
    turned = jnp.concatenate([queries[:, HD // 2:], queries[:, :HD // 2]], axis=1)
    queries = (queries * cos_q[...] + turned * sin_q[...]).astype(BF16)

    share = HD // T
    shift = share.bit_length() - 1
    feature = lax.broadcasted_iota(jnp.int32, (HD, T * KC), 0)
    column = lax.broadcasted_iota(jnp.int32, (HD, T * KC), 1)
    source = (feature >> shift) * KC + (feature & (share - 1)) + (me // GROUP) * (2 * share)
    key_picks = (column == source).astype(F32).astype(BF16)
    value_picks = (column == source + share).astype(F32).astype(BF16)

    each_peer(lambda peer: kv_copy(peer, peer).wait_recv())
    everything = kvall[...].reshape(T * KC, L)
    keys = jnp.dot(key_picks, everything, preferred_element_type=F32)
    values = jnp.dot(value_picks, everything, preferred_element_type=F32).astype(BF16)
    turned = jnp.concatenate([keys[HD // 2:], keys[:HD // 2]], axis=0)
    keys = (keys * cos_k[...] + turned * sin_k[...]).astype(BF16)
    for c in range(2):
        seen = (c + 1) * half
        scores = jnp.dot(queries[c * half:seen], keys[:, :seen], preferred_element_type=F32) * (HD ** -0.5)
        before = lax.broadcasted_iota(jnp.int32, (half, seen), 0) + c * half >= lax.broadcasted_iota(
            jnp.int32, (half, seen), 1
        )
        scores = jnp.where(before, scores, -1e30)
        weights = jnp.exp(scores - jnp.max(scores, axis=1, keepdims=True))
        weights = (weights * (1.0 / jnp.sum(weights, axis=1, keepdims=True))).astype(BF16)
        out[half_rows(c), :] = dot_nt(weights, values[:, :seen]).astype(BF16)

    def drain(k, c):
        for side, g in pairs_of:
            rs_copy(side, g, k + 1, first.at[rows(g)]).wait_send()
            ag_copy(side, g, k, me).wait_send()
        return c

    lax.fori_loop(0, H - 1, drain, 0)
    for side, g in pairs_of:
        if is_long(side, g):
            rs_copy(side, g, H, first.at[rows(g)]).wait_send()
            ag_copy(side, g, H - 1, me).wait_send()
    for g in range(NG):
        shift_copy(g).wait_send()
    each_peer(lambda peer: gain_copy(peer, me).wait_send())
    each_peer(lambda peer: kv_copy(peer, me).wait_send())


def on_device(context, out_weight, residual, gain, q_weight, kv_weight):
    T = lax.axis_size("tensor")
    S = lax.axis_size("section")
    _, L, HD = context.shape
    B = residual.shape[2]
    D = out_weight.shape[2]
    KC = kv_weight.shape[2]
    tables = rope_tables(L, HD)
    vmem = pl.BlockSpec(memory_space=pltpu.VMEM)
    anywhere = pl.BlockSpec(memory_space=pl.ANY)
    dma = pltpu.SemaphoreType.DMA
    attended = pl.pallas_call(
        functools.partial(kernel, T, S),
        out_shape=jax.ShapeDtypeStruct((L, HD), BF16),
        in_specs=[vmem] * 7 + [anywhere] * 3,
        out_specs=vmem,
        scratch_shapes=[
            pltpu.VMEM((HD, D), BF16),
            pltpu.VMEM((KC, D), BF16),
            pltpu.VMEM((D, 2 * HD), BF16),
            pltpu.VMEM((L, B), BF16),
            pltpu.VMEM((2, T // 2, L, B), BF16),
            pltpu.VMEM((L, B), BF16),
            pltpu.VMEM((T, L, B), BF16),
            pltpu.VMEM((T, 1, B), F32),
            pltpu.VMEM((L, 2 * HD), F32),
            pltpu.VMEM((L, HD), F32),
            pltpu.VMEM((T, KC, L), BF16),
            pltpu.VMEM((2, L, B), F32),
            dma((T,)), dma((2,)),
            dma((2, NG, T // 2)), dma((2, NG, T // 2)),
            dma((NG,)), dma((NG,)),
            dma((2, NG, T // 2)), dma((2, NG, T // 2)),
            dma((T,)), dma((T,)),
            dma((T,)), dma((T,)),
        ],
        compiler_params=pltpu.CompilerParams(
            collective_id=0, has_side_effects=True, vmem_limit_bytes=62 * 2**20
        ),
        cost_estimate=pl.CostEstimate(
            flops=2 * L * D * HD * 3, bytes_accessed=D * HD * 6, transcendentals=L * L
        ),
        name="handover_attention",
    )(
        context[0], residual[0], gain, *[jnp.asarray(t) for t in tables],
        out_weight[0], q_weight[0], jnp.swapaxes(kv_weight[0], 0, 1),
    )
    return attended[None]


def solution(mesh):
    placed = (
        P("section", None, "tensor"),
        P("section", "tensor", None),
        P("section", None, "tensor"),
        P("section", "tensor"),
        P("section", None, "tensor"),
        P("section", None, "tensor"),
    )
    return jax.shard_map(
        on_device,
        mesh=mesh,
        in_specs=placed,
        out_specs=P("section", None, "tensor"),
        check_vma=False,
    )
```

```python
import functools

import jax
import jax.numpy as jnp
import numpy as np
from jax import lax
from jax.experimental import pallas as pl
from jax.experimental.pallas import tpu as pltpu
from jax.sharding import PartitionSpec as P

GROUP = 8
THETA = 500000.0
EPS = 1e-05
MESH = pl.DeviceIdType.MESH
BF16 = jnp.bfloat16
F32 = jnp.float32
NG = 8


def rope_tables(length, head_size):
    half = head_size // 2
    frequency = np.float32(THETA) ** (-(np.arange(half, dtype=np.float32) * np.float32(2.0) / np.float32(head_size)))
    angles = np.arange(length, dtype=np.float32)[:, None] * frequency.astype(np.float32)[None, :]
    cosine, sine = np.cos(angles).astype(np.float32), np.sin(angles).astype(np.float32)
    return (
        np.concatenate([cosine, cosine], axis=1),
        np.concatenate([-sine, sine], axis=1),
        np.ascontiguousarray(np.concatenate([cosine, cosine], axis=1).T),
        np.ascontiguousarray(np.concatenate([-sine, sine], axis=1).T),
    )


def dot_nt(a, b):
    return lax.dot_general(a, b, (((1,), (1,)), ((), ())), preferred_element_type=F32)


def kernel(
    T, S,
    ctx, res, gain, cos_q, sin_q, cos_k, sin_k, ow_hbm, qw_hbm, kvw_hbm,
    out,
    ow, kvw, w, first, rs, hand, xb, gains, acc, ssq, kvall, terms,
    ow_sem, load_sem, rs_send, rs_recv, sh_send, sh_recv, ag_send, ag_recv, g_send, g_recv, kv_send, kv_recv,
):
    L, HD = ctx.shape
    B = res.shape[1]
    D = ow.shape[1]
    KC = kvw.shape[0]
    R = L // NG
    H = T // 2
    half = L // 2
    sec = lax.axis_index("section")
    me = lax.axis_index("tensor")

    def ring(pos):
        upper = pos // (T // 2)
        return (1 - upper) * (2 * pos) + upper * (2 * (T - 1 - pos) + 1)

    y = me % 2
    p = (1 - y) * (me // 2) + y * (T - 1 - me // 2)

    def at(offset):
        return ring((p + offset + 2 * T) % T)

    sides = (at(1), at(-1))
    signs = (1, -1)
    following = (sec + 1) % S
    previous = (sec + S - 1) % S

    def block(owner):
        return pl.ds(pl.multiple_of(owner * B, B), B)

    def ow_copy(owner):
        return pltpu.make_async_copy(ow_hbm.at[:, block(owner)], ow.at[:, block(owner)], ow_sem.at[owner])

    ow_copy(at(H)).start()
    ow_copy(at(H - 1)).start()
    ow_copy(at(1 - H)).start()

    def load_rest(j, c):
        ow_copy(at(j)).start()
        return c

    def wait_rest(j, c):
        ow_copy(at(j)).wait()
        return c

    lax.fori_loop(T + 2 - H, T + H - 1, load_rest, 0)
    kv_load = pltpu.make_async_copy(kvw_hbm, kvw, load_sem.at[0])
    kv_load.start()
    q_load = pltpu.make_async_copy(qw_hbm, w.at[:, pl.ds(0, HD)], load_sem.at[1])
    q_load.start()

    barrier = pltpu.get_barrier_semaphore()

    def each_peer(act):
        def step(j, c):
            act((me + j) % T)
            return c

        lax.fori_loop(1, T, step, 0)

    def greet(s, t):
        pl.semaphore_signal(barrier, inc=1, device_id=(s, t), device_id_type=MESH)

    each_peer(lambda peer: greet(sec, peer))
    greet(following, me)
    greet(previous, me)

    def rows(g):
        return pl.ds(g * R, R)

    def is_long(side, g):
        return (g // (NG // 2)) == side

    order = [g for j in range(NG // 2) for g in (j, j + NG // 2)]
    pairs_of = [(side, g) for g in order for side in range(2)]

    def rs_copy(side, g, left, source):
        return pltpu.make_async_remote_copy(
            src_ref=source, dst_ref=rs.at[side, left - 1, rows(g)],
            send_sem=rs_send.at[side, g, left - 1], recv_sem=rs_recv.at[side, g, left - 1],
            device_id=(sec, sides[side]), device_id_type=MESH,
        )

    def shift_copy(g):
        return pltpu.make_async_remote_copy(
            src_ref=hand.at[rows(g)], dst_ref=xb.at[me, rows(g)], send_sem=sh_send.at[g], recv_sem=sh_recv.at[g],
            device_id=(following, me), device_id_type=MESH,
        )

    def ag_copy(side, g, k, owner):
        return pltpu.make_async_remote_copy(
            src_ref=xb.at[owner, rows(g)], dst_ref=xb.at[owner, rows(g)],
            send_sem=ag_send.at[side, g, k], recv_sem=ag_recv.at[side, g, k],
            device_id=(sec, sides[side]), device_id_type=MESH,
        )

    def gain_copy(peer, slot):
        return pltpu.make_async_remote_copy(
            src_ref=gain, dst_ref=gains.at[slot], send_sem=g_send.at[peer], recv_sem=g_recv.at[slot],
            device_id=(sec, peer), device_id_type=MESH,
        )

    def kv_copy(peer, slot):
        return pltpu.make_async_remote_copy(
            src_ref=kvall.at[me], dst_ref=kvall.at[slot], send_sem=kv_send.at[peer], recv_sem=kv_recv.at[slot],
            device_id=(sec, peer), device_id_type=MESH,
        )

    def half_rows(side):
        return pl.ds(side * half, half)

    def term(owner):
        return jnp.dot(ctx[...], ow[:, block(owner)], preferred_element_type=F32)

    def project(owner):
        features = xb[owner].astype(F32)
        scaled = (features * gains[owner]).astype(BF16)
        squares = features * features
        total = squares[:, :HD]
        for i in range(1, B // HD):
            total = total + squares[:, i * HD:(i + 1) * HD]
        ssq[...] += total
        acc[...] += jnp.dot(scaled, w[block(owner), :], preferred_element_type=F32)

    def place(i):
        w[block(i), HD:] = jnp.concatenate(
            [jnp.transpose(kvw[:, block(i)]), jnp.zeros((B, HD - KC), BF16)], axis=1
        )

    ow_copy(at(H)).wait()
    first[...] = term(at(H)).astype(BF16)
    pl.semaphore_wait(barrier, T + 1)
    for side, g in pairs_of:
        if is_long(side, g):
            rs_copy(side, g, H, first.at[rows(g)]).start()

    for side in range(2):
        ow_copy(at(signs[side] * (H - 1))).wait()
        terms[side] = term(at(signs[side] * (H - 1)))
    for side, g in pairs_of:
        if not is_long(side, g):
            rs[side, H - 1, rows(g), :] = terms[side, rows(g), :].astype(BF16)
            rs_copy(side, g, H - 1, rs.at[side, H - 1, rows(g)]).start()
    gains[me] = gain[...]
    each_peer(lambda peer: gain_copy(peer, me).start())

    for side, g in pairs_of:
        if is_long(side, g):
            rs_copy(side, g, H, first.at[rows(g)]).wait_recv()
            total = rs[side, H - 1, rows(g), :].astype(F32) + terms[side, rows(g), :]
            rs[side, H - 1, rows(g), :] = total.astype(BF16)
            rs_copy(side, g, H - 1, rs.at[side, H - 1, rows(g)]).start()

    lax.fori_loop(T + 2 - H, T + H - 1, wait_rest, 0)
    for side in range(2):
        terms[side] = term(at(signs[side] * (H - 2)))
    acc[...] = jnp.zeros_like(acc)
    ssq[...] = jnp.zeros_like(ssq)
    kv_load.wait()
    place(T - 2)
    place(T - 1)

    def reduce_step(i, c):
        left = H - 2 - i
        for side, g in pairs_of:
            rs_copy(side, g, left + 1, first.at[rows(g)]).wait_recv()
            total = rs[side, left, rows(g), :].astype(F32) + terms[side, rows(g), :]
            rs[side, left, rows(g), :] = total.astype(BF16)
            rs_copy(side, g, left, rs.at[side, left, rows(g)]).start()
        for side in range(2):
            terms[side] = term(at(signs[side] * (left - 1)))
        for n in range(2):
            place(2 * i + n)
        return c

    lax.fori_loop(0, H - 2, reduce_step, 0)
    terms[0] += res[...].astype(F32)
    for g in order:
        for side in range(2):
            rs_copy(side, g, 1, first.at[rows(g)]).wait_recv()
        total = rs[0, 0, rows(g), :].astype(F32) + rs[1, 0, rows(g), :].astype(F32) + terms[0, rows(g), :]
        hand[rows(g), :] = total.astype(BF16)
        shift_copy(g).start()
    place(T - 4)
    place(T - 3)

    each_peer(lambda peer: gain_copy(peer, peer).wait_recv())
    q_load.wait()
    for g in order:
        shift_copy(g).wait_recv()
        for side in range(2):
            ag_copy(side, g, 0, me).start()
    project(me)

    def gather_step(k, c):
        owners = [at(-signs[side] * (1 + k)) for side in range(2)]
        for side, g in pairs_of:
            ag_copy(side, g, k, owners[side]).wait_recv()
            ag_copy(side, g, k + 1, owners[side]).start()
        for side in range(2):
            project(owners[side])
        return c

    lax.fori_loop(0, H - 2, gather_step, 0)
    owners = [at(-signs[side] * (H - 1)) for side in range(2)]
    for wanted in (True, False):
        for side, g in pairs_of:
            if is_long(side, g) == wanted:
                ag_copy(side, g, H - 2, owners[side]).wait_recv()
                if wanted:
                    ag_copy(side, g, H - 1, owners[side]).start()
    for side in range(2):
        project(owners[side])
    for side, g in pairs_of:
        if is_long(side, g):
            ag_copy(side, g, H - 1, at(H)).wait_recv()
    project(at(H))

    factor = lax.rsqrt(jnp.sum(ssq[...], axis=1, keepdims=True) * (1.0 / D) + EPS)
    pairs = (acc[:, HD:] * factor).astype(BF16)
    eye = lax.broadcasted_iota(jnp.int32, (KC, HD), 0) == lax.broadcasted_iota(jnp.int32, (KC, HD), 1)
    kvall[me] = dot_nt(eye.astype(F32).astype(BF16), pairs).astype(BF16)
    each_peer(lambda peer: kv_copy(peer, me).start())

    queries = acc[:, :HD] * factor
    turned = jnp.concatenate([queries[:, HD // 2:], queries[:, :HD // 2]], axis=1)
    queries = (queries * cos_q[...] + turned * sin_q[...]).astype(BF16)

    share = HD // T
    shift = share.bit_length() - 1
    feature = lax.broadcasted_iota(jnp.int32, (HD, T * KC), 0)
    column = lax.broadcasted_iota(jnp.int32, (HD, T * KC), 1)
    source = (feature >> shift) * KC + (feature & (share - 1)) + (me // GROUP) * (2 * share)
    key_picks = (column == source).astype(F32).astype(BF16)
    value_picks = (column == source + share).astype(F32).astype(BF16)

    each_peer(lambda peer: kv_copy(peer, peer).wait_recv())
    everything = kvall[...].reshape(T * KC, L)
    keys = jnp.dot(key_picks, everything, preferred_element_type=F32)
    values = jnp.dot(value_picks, everything, preferred_element_type=F32).astype(BF16)
    turned = jnp.concatenate([keys[HD // 2:], keys[:HD // 2]], axis=0)
    keys = (keys * cos_k[...] + turned * sin_k[...]).astype(BF16)
    for c in range(2):
        seen = (c + 1) * half
        scores = jnp.dot(queries[c * half:seen], keys[:, :seen], preferred_element_type=F32) * (HD ** -0.5)
        before = lax.broadcasted_iota(jnp.int32, (half, seen), 0) + c * half >= lax.broadcasted_iota(
            jnp.int32, (half, seen), 1
        )
        scores = jnp.where(before, scores, -1e30)
        weights = jnp.exp(scores - jnp.max(scores, axis=1, keepdims=True))
        weights = (weights * (1.0 / jnp.sum(weights, axis=1, keepdims=True))).astype(BF16)
        out[half_rows(c), :] = dot_nt(weights, values[:, :seen]).astype(BF16)

    def drain(k, c):
        for side, g in pairs_of:
            rs_copy(side, g, k + 1, first.at[rows(g)]).wait_send()
            ag_copy(side, g, k, me).wait_send()
        return c

    lax.fori_loop(0, H - 1, drain, 0)
    for side, g in pairs_of:
        if is_long(side, g):
            rs_copy(side, g, H, first.at[rows(g)]).wait_send()
            ag_copy(side, g, H - 1, me).wait_send()
    for g in range(NG):
        shift_copy(g).wait_send()
    each_peer(lambda peer: gain_copy(peer, me).wait_send())
    each_peer(lambda peer: kv_copy(peer, me).wait_send())


def on_device(context, out_weight, residual, gain, q_weight, kv_weight):
    T = lax.axis_size("tensor")
    S = lax.axis_size("section")
    _, L, HD = context.shape
    B = residual.shape[2]
    D = out_weight.shape[2]
    KC = kv_weight.shape[2]
    tables = rope_tables(L, HD)
    vmem = pl.BlockSpec(memory_space=pltpu.VMEM)
    anywhere = pl.BlockSpec(memory_space=pl.ANY)
    dma = pltpu.SemaphoreType.DMA
    attended = pl.pallas_call(
        functools.partial(kernel, T, S),
        out_shape=jax.ShapeDtypeStruct((L, HD), BF16),
        in_specs=[vmem] * 7 + [anywhere] * 3,
        out_specs=vmem,
        scratch_shapes=[
            pltpu.VMEM((HD, D), BF16),
            pltpu.VMEM((KC, D), BF16),
            pltpu.VMEM((D, 2 * HD), BF16),
            pltpu.VMEM((L, B), BF16),
            pltpu.VMEM((2, T // 2, L, B), BF16),
            pltpu.VMEM((L, B), BF16),
            pltpu.VMEM((T, L, B), BF16),
            pltpu.VMEM((T, 1, B), F32),
            pltpu.VMEM((L, 2 * HD), F32),
            pltpu.VMEM((L, HD), F32),
            pltpu.VMEM((T, KC, L), BF16),
            pltpu.VMEM((2, L, B), F32),
            dma((T,)), dma((2,)),
            dma((2, NG, T // 2)), dma((2, NG, T // 2)),
            dma((NG,)), dma((NG,)),
            dma((2, NG, T // 2)), dma((2, NG, T // 2)),
            dma((T,)), dma((T,)),
            dma((T,)), dma((T,)),
        ],
        compiler_params=pltpu.CompilerParams(
            collective_id=0, has_side_effects=True, vmem_limit_bytes=52 * 2**20
        ),
        cost_estimate=pl.CostEstimate(
            flops=2 * L * D * HD * 3, bytes_accessed=D * HD * 6, transcendentals=L * L
        ),
        name="handover_attention",
    )(
        context[0], residual[0], gain, *[jnp.asarray(t) for t in tables],
        out_weight[0], q_weight[0], jnp.swapaxes(kv_weight[0], 0, 1),
    )
    return attended[None]


def solution(mesh):
    placed = (
        P("section", None, "tensor"),
        P("section", "tensor", None),
        P("section", None, "tensor"),
        P("section", "tensor"),
        P("section", None, "tensor"),
        P("section", None, "tensor"),
    )
    return jax.shard_map(
        on_device,
        mesh=mesh,
        in_specs=placed,
        out_specs=P("section", None, "tensor"),
        check_vma=False,
    )
```

```python
import functools

import jax
import jax.numpy as jnp
import numpy as np
from jax import lax
from jax.experimental import pallas as pl
from jax.experimental.pallas import tpu as pltpu
from jax.sharding import PartitionSpec as P

GROUP = 8
THETA = 500000.0
EPS = 1e-05
MESH = pl.DeviceIdType.MESH
BF16 = jnp.bfloat16
F32 = jnp.float32
NG = 4


def rope_tables(length, head_size):
    half = head_size // 2
    frequency = np.float32(THETA) ** (-(np.arange(half, dtype=np.float32) * np.float32(2.0) / np.float32(head_size)))
    angles = np.arange(length, dtype=np.float32)[:, None] * frequency.astype(np.float32)[None, :]
    cosine, sine = np.cos(angles).astype(np.float32), np.sin(angles).astype(np.float32)
    return (
        np.concatenate([cosine, cosine], axis=1),
        np.concatenate([-sine, sine], axis=1),
        np.ascontiguousarray(np.concatenate([cosine, cosine], axis=1).T),
        np.ascontiguousarray(np.concatenate([-sine, sine], axis=1).T),
    )


def dot_nt(a, b):
    return lax.dot_general(a, b, (((1,), (1,)), ((), ())), preferred_element_type=F32)


def kernel(
    T, S,
    ctx_hbm, res_hbm, gain_hbm, cos_q_hbm, sin_q_hbm, cos_k_hbm, sin_k_hbm, ow_hbm, qw_hbm, kvw_hbm,
    out,
    ctx, res, cos_q, sin_q, cos_k, sin_k,
    ow, kvw, w, first, rs, hand, base, xb, gains, acc, ssq, kvall, terms,
    ow_sem, load_sem, rs_send, rs_recv, sh_send, sh_recv, ag_send, ag_recv, g_send, g_recv, kv_send, kv_recv,
):
    L, HD = ctx.shape
    B = res.shape[1]
    D = ow.shape[1]
    KC = kvw.shape[0]
    R = L // NG
    H = T // 2
    half = L // 2
    sec = lax.axis_index("section")
    me = lax.axis_index("tensor")

    def ring(pos):
        upper = pos // (T // 2)
        return (1 - upper) * (2 * pos) + upper * (2 * (T - 1 - pos) + 1)

    y = me % 2
    p = (1 - y) * (me // 2) + y * (T - 1 - me // 2)

    def at(offset):
        return ring((p + offset + 2 * T) % T)

    sides = (at(1), at(-1))
    signs = (1, -1)
    following = (sec + 1) % S
    previous = (sec + S - 1) % S

    def block(owner):
        return pl.ds(pl.multiple_of(owner * B, B), B)

    def ow_copy(owner):
        return pltpu.make_async_copy(ow_hbm.at[:, block(owner)], ow.at[:, block(owner)], ow_sem.at[owner])

    ctx_load = pltpu.make_async_copy(ctx_hbm, ctx, load_sem.at[2])
    ctx_load.start()
    ow_copy(at(H)).start()
    ow_copy(at(H - 1)).start()
    ow_copy(at(1 - H)).start()

    def load_rest(j, c):
        ow_copy(at(j)).start()
        return c

    def wait_rest(j, c):
        ow_copy(at(j)).wait()
        return c

    lax.fori_loop(T + 2 - H, T + H - 1, load_rest, 0)
    kv_load = pltpu.make_async_copy(kvw_hbm, kvw, load_sem.at[0])
    kv_load.start()
    q_load = pltpu.make_async_copy(qw_hbm, w.at[:, pl.ds(0, HD)], load_sem.at[1])
    q_load.start()

    gain_load = pltpu.make_async_copy(gain_hbm, gains.at[me], load_sem.at[3])
    gain_load.start()
    res_load = pltpu.make_async_copy(res_hbm, res, load_sem.at[4])
    res_load.start()
    table_loads = [
        pltpu.make_async_copy(source, target, load_sem.at[5 + i])
        for i, (source, target) in enumerate(
            ((cos_q_hbm, cos_q), (sin_q_hbm, sin_q), (cos_k_hbm, cos_k), (sin_k_hbm, sin_k))
        )
    ]
    for load in table_loads:
        load.start()

    barrier = pltpu.get_barrier_semaphore()

    def each_peer(act):
        def step(j, c):
            act((me + j) % T)
            return c

        lax.fori_loop(1, T, step, 0)

    def greet(s, t):
        pl.semaphore_signal(barrier, inc=1, device_id=(s, t), device_id_type=MESH)

    each_peer(lambda peer: greet(sec, peer))
    for section in (following, previous):
        greet(section, me)
        for side in range(2):
            greet(section, sides[side])

    def rows(g):
        return pl.ds(g * R, R)

    def is_long(side, g):
        return (g // (NG // 2)) == side

    order = [g for j in range(NG // 2) for g in (j, j + NG // 2)]
    pairs_of = [(side, g) for g in order for side in range(2)]

    def rs_copy(side, g, left, source, section=None):
        return pltpu.make_async_remote_copy(
            src_ref=source, dst_ref=rs.at[side, left - 1, rows(g)],
            send_sem=rs_send.at[side, g, left - 1], recv_sem=rs_recv.at[side, g, left - 1],
            device_id=(sec if section is None else section, sides[side]), device_id_type=MESH,
        )

    def shift_copy(g):
        return pltpu.make_async_remote_copy(
            src_ref=hand.at[rows(g)], dst_ref=base.at[rows(g)], send_sem=sh_send.at[g], recv_sem=sh_recv.at[g],
            device_id=(following, me), device_id_type=MESH,
        )

    def ag_copy(side, g, k, owner):
        return pltpu.make_async_remote_copy(
            src_ref=xb.at[owner, rows(g)], dst_ref=xb.at[owner, rows(g)],
            send_sem=ag_send.at[side, g, k], recv_sem=ag_recv.at[side, g, k],
            device_id=(sec, sides[side]), device_id_type=MESH,
        )

    def gain_copy(peer, slot):
        return pltpu.make_async_remote_copy(
            src_ref=gains.at[me], dst_ref=gains.at[slot], send_sem=g_send.at[peer], recv_sem=g_recv.at[slot],
            device_id=(sec, peer), device_id_type=MESH,
        )

    def kv_copy(peer, slot):
        return pltpu.make_async_remote_copy(
            src_ref=kvall.at[me], dst_ref=kvall.at[slot], send_sem=kv_send.at[peer], recv_sem=kv_recv.at[slot],
            device_id=(sec, peer), device_id_type=MESH,
        )

    def half_rows(side):
        return pl.ds(side * half, half)

    def term(owner):
        return jnp.dot(ctx[...], ow[:, block(owner)], preferred_element_type=F32)

    def project(owner):
        features = xb[owner].astype(F32)
        scaled = (features * gains[owner]).astype(BF16)
        squares = features * features
        total = squares[:, :HD]
        for i in range(1, B // HD):
            total = total + squares[:, i * HD:(i + 1) * HD]
        ssq[...] += total
        acc[...] += jnp.dot(scaled, w[block(owner), :], preferred_element_type=F32)

    def place(i):
        w[block(i), HD:] = jnp.concatenate(
            [jnp.transpose(kvw[:, block(i)]), jnp.zeros((B, HD - KC), BF16)], axis=1
        )

    ctx_load.wait()
    ow_copy(at(H)).wait()
    first[...] = term(at(H)).astype(BF16)
    pl.semaphore_wait(barrier, T + 5)
    for side, g in pairs_of:
        if is_long(side, g):
            rs_copy(side, g, H, first.at[rows(g)]).start()

    for side in range(2):
        ow_copy(at(signs[side] * (H - 1))).wait()
        terms[side] = term(at(signs[side] * (H - 1)))
    for side, g in pairs_of:
        if not is_long(side, g):
            rs[side, H - 1, rows(g), :] = terms[side, rows(g), :].astype(BF16)
            rs_copy(side, g, H - 1, rs.at[side, H - 1, rows(g)]).start()
    gain_load.wait()
    each_peer(lambda peer: gain_copy(peer, me).start())

    for side, g in pairs_of:
        if is_long(side, g):
            rs_copy(side, g, H, first.at[rows(g)]).wait_recv()
            total = rs[side, H - 1, rows(g), :].astype(F32) + terms[side, rows(g), :]
            rs[side, H - 1, rows(g), :] = total.astype(BF16)
            rs_copy(side, g, H - 1, rs.at[side, H - 1, rows(g)]).start()

    lax.fori_loop(T + 2 - H, T + H - 1, wait_rest, 0)
    for side in range(2):
        terms[side] = term(at(signs[side] * (H - 2)))
    res_load.wait()
    hand[...] = (term(me) + res[...].astype(F32)).astype(BF16)
    for g in order:
        shift_copy(g).start()
    acc[...] = jnp.zeros_like(acc)
    ssq[...] = jnp.zeros_like(ssq)
    kv_load.wait()
    place(T - 2)
    place(T - 1)

    def pass_sums(left, section=None):
        for side, g in pairs_of:
            rs_copy(side, g, left + 1, first.at[rows(g)]).wait_recv()
            total = rs[side, left, rows(g), :].astype(F32) + terms[side, rows(g), :]
            rs[side, left, rows(g), :] = total.astype(BF16)
            rs_copy(side, g, left, rs.at[side, left, rows(g)], section).start()

    def reduce_step(i, c):
        left = H - 2 - i
        pass_sums(left)
        for side in range(2):
            terms[side] = term(at(signs[side] * (left - 1)))
        for n in range(2):
            place(2 * i + n)
        return c

    lax.fori_loop(0, H - 3, reduce_step, 0)
    pass_sums(1, following)
    for i in range(T - 6, T - 2):
        place(i)

    each_peer(lambda peer: gain_copy(peer, peer).wait_recv())
    q_load.wait()
    for load in table_loads:
        load.wait()
    for g in order:
        shift_copy(g).wait_recv()
        for side in range(2):
            rs_copy(side, g, 1, first.at[rows(g)], following).wait_recv()
        total = base[rows(g), :].astype(F32) + rs[0, 0, rows(g), :].astype(F32) + rs[1, 0, rows(g), :].astype(F32)
        xb[me, rows(g), :] = total.astype(BF16)
        for side in range(2):
            ag_copy(side, g, 0, me).start()
    project(me)

    def gather_step(k, c):
        owners = [at(-signs[side] * (1 + k)) for side in range(2)]
        for side, g in pairs_of:
            ag_copy(side, g, k, owners[side]).wait_recv()
            ag_copy(side, g, k + 1, owners[side]).start()
        for side in range(2):
            project(owners[side])
        return c

    lax.fori_loop(0, H - 2, gather_step, 0)
    owners = [at(-signs[side] * (H - 1)) for side in range(2)]
    for wanted in (True, False):
        for side, g in pairs_of:
            if is_long(side, g) == wanted:
                ag_copy(side, g, H - 2, owners[side]).wait_recv()
                if wanted:
                    ag_copy(side, g, H - 1, owners[side]).start()
    for side in range(2):
        project(owners[side])
    for side, g in pairs_of:
        if is_long(side, g):
            ag_copy(side, g, H - 1, at(H)).wait_recv()
    project(at(H))

    factor = lax.rsqrt(jnp.sum(ssq[...], axis=1, keepdims=True) * (1.0 / D) + EPS)
    pairs = (acc[:, HD:] * factor).astype(BF16)
    eye = lax.broadcasted_iota(jnp.int32, (KC, HD), 0) == lax.broadcasted_iota(jnp.int32, (KC, HD), 1)
    kvall[me] = dot_nt(eye.astype(F32).astype(BF16), pairs).astype(BF16)
    each_peer(lambda peer: kv_copy(peer, me).start())

    queries = acc[:, :HD] * factor
    turned = jnp.concatenate([queries[:, HD // 2:], queries[:, :HD // 2]], axis=1)
    queries = (queries * cos_q[...] + turned * sin_q[...]).astype(BF16)

    share = HD // T
    shift = share.bit_length() - 1
    feature = lax.broadcasted_iota(jnp.int32, (HD, T * KC), 0)
    column = lax.broadcasted_iota(jnp.int32, (HD, T * KC), 1)
    source = (feature >> shift) * KC + (feature & (share - 1)) + (me // GROUP) * (2 * share)
    key_picks = (column == source).astype(F32).astype(BF16)
    value_picks = (column == source + share).astype(F32).astype(BF16)

    each_peer(lambda peer: kv_copy(peer, peer).wait_recv())
    everything = kvall[...].reshape(T * KC, L)
    keys = jnp.dot(key_picks, everything, preferred_element_type=F32)
    values = jnp.dot(value_picks, everything, preferred_element_type=F32).astype(BF16)
    turned = jnp.concatenate([keys[HD // 2:], keys[:HD // 2]], axis=0)
    keys = (keys * cos_k[...] + turned * sin_k[...]).astype(BF16)
    for c in range(2):
        seen = (c + 1) * half
        scores = jnp.dot(queries[c * half:seen], keys[:, :seen], preferred_element_type=F32) * (HD ** -0.5)
        before = lax.broadcasted_iota(jnp.int32, (half, seen), 0) + c * half >= lax.broadcasted_iota(
            jnp.int32, (half, seen), 1
        )
        scores = jnp.where(before, scores, -1e30)
        weights = jnp.exp(scores - jnp.max(scores, axis=1, keepdims=True))
        weights = (weights * (1.0 / jnp.sum(weights, axis=1, keepdims=True))).astype(BF16)
        out[half_rows(c), :] = dot_nt(weights, values[:, :seen]).astype(BF16)

    def drain(k, c):
        for side, g in pairs_of:
            rs_copy(side, g, k + 1, first.at[rows(g)]).wait_send()
            ag_copy(side, g, k, me).wait_send()
        return c

    lax.fori_loop(0, H - 1, drain, 0)
    for side, g in pairs_of:
        if is_long(side, g):
            rs_copy(side, g, H, first.at[rows(g)]).wait_send()
            ag_copy(side, g, H - 1, me).wait_send()
    for g in range(NG):
        shift_copy(g).wait_send()
    each_peer(lambda peer: gain_copy(peer, me).wait_send())
    each_peer(lambda peer: kv_copy(peer, me).wait_send())


def on_device(context, out_weight, residual, gain, q_weight, kv_weight):
    T = lax.axis_size("tensor")
    S = lax.axis_size("section")
    _, L, HD = context.shape
    B = residual.shape[2]
    D = out_weight.shape[2]
    KC = kv_weight.shape[2]
    tables = rope_tables(L, HD)
    vmem = pl.BlockSpec(memory_space=pltpu.VMEM)
    hbm = pl.BlockSpec(memory_space=pltpu.HBM)
    dma = pltpu.SemaphoreType.DMA
    attended = pl.pallas_call(
        functools.partial(kernel, T, S),
        out_shape=jax.ShapeDtypeStruct((L, HD), BF16),
        in_specs=[hbm] * 10,
        out_specs=vmem,
        scratch_shapes=[
            pltpu.VMEM((L, HD), BF16),
            pltpu.VMEM((L, B), BF16),
            pltpu.VMEM((L, HD), F32),
            pltpu.VMEM((L, HD), F32),
            pltpu.VMEM((HD, L), F32),
            pltpu.VMEM((HD, L), F32),
            pltpu.VMEM((HD, D), BF16),
            pltpu.VMEM((KC, D), BF16),
            pltpu.VMEM((D, 2 * HD), BF16),
            pltpu.VMEM((L, B), BF16),
            pltpu.VMEM((2, T // 2, L, B), BF16),
            pltpu.VMEM((L, B), BF16),
            pltpu.VMEM((L, B), BF16),
            pltpu.VMEM((T, L, B), BF16),
            pltpu.VMEM((T, 1, B), F32),
            pltpu.VMEM((L, 2 * HD), F32),
            pltpu.VMEM((L, HD), F32),
            pltpu.VMEM((T, KC, L), BF16),
            pltpu.VMEM((2, L, B), F32),
            dma((T,)), dma((9,)),
            dma((2, NG, T // 2)), dma((2, NG, T // 2)),
            dma((NG,)), dma((NG,)),
            dma((2, NG, T // 2)), dma((2, NG, T // 2)),
            dma((T,)), dma((T,)),
            dma((T,)), dma((T,)),
        ],
        compiler_params=pltpu.CompilerParams(
            collective_id=0, has_side_effects=True, vmem_limit_bytes=62 * 2**20
        ),
        cost_estimate=pl.CostEstimate(
            flops=2 * L * D * HD * 3, bytes_accessed=D * HD * 6, transcendentals=L * L
        ),
        name="handover_attention",
    )(
        context[0], residual[0], gain, *[jnp.asarray(t) for t in tables],
        out_weight[0], q_weight[0], jnp.swapaxes(kv_weight[0], 0, 1),
    )
    return attended[None]


def solution(mesh):
    placed = (
        P("section", None, "tensor"),
        P("section", "tensor", None),
        P("section", None, "tensor"),
        P("section", "tensor"),
        P("section", None, "tensor"),
        P("section", None, "tensor"),
    )
    return jax.shard_map(
        on_device,
        mesh=mesh,
        in_specs=placed,
        out_specs=P("section", None, "tensor"),
        check_vma=False,
    )
```

```python
import functools

import jax
import jax.numpy as jnp
import numpy as np
from jax import lax
from jax.experimental import pallas as pl
from jax.experimental.pallas import tpu as pltpu
from jax.sharding import PartitionSpec as P

GROUP = 8
THETA = 500000.0
EPS = 1e-05
MESH = pl.DeviceIdType.MESH
BF16 = jnp.bfloat16
F32 = jnp.float32
NG = 4


def rope_tables(length, head_size):
    half = head_size // 2
    frequency = np.float32(THETA) ** (-(np.arange(half, dtype=np.float32) * np.float32(2.0) / np.float32(head_size)))
    angles = np.arange(length, dtype=np.float32)[:, None] * frequency.astype(np.float32)[None, :]
    cosine, sine = np.cos(angles).astype(np.float32), np.sin(angles).astype(np.float32)
    return (
        np.concatenate([cosine, cosine], axis=1),
        np.concatenate([-sine, sine], axis=1),
        np.ascontiguousarray(np.concatenate([cosine, cosine], axis=1).T),
        np.ascontiguousarray(np.concatenate([-sine, sine], axis=1).T),
    )


def dot_nt(a, b):
    return lax.dot_general(a, b, (((1,), (1,)), ((), ())), preferred_element_type=F32)


def kernel(
    T, S,
    ctx_hbm, res_hbm, gain_hbm, cos_q_hbm, sin_q_hbm, cos_k_hbm, sin_k_hbm, ow_hbm, qw_hbm, kvw_hbm,
    out,
    ctx, res, cos_q, sin_q, cos_k, sin_k,
    ow, kvw, w, first, rs, hand, base, xb, gains, acc, ssq, kvall, terms,
    ow_sem, load_sem, rs_send, rs_recv, sh_send, sh_recv, ag_send, ag_recv, g_send, g_recv, kv_send, kv_recv,
):
    L, HD = ctx.shape
    B = res.shape[1]
    D = ow.shape[1]
    KC = kvw.shape[0]
    R = L // NG
    H = T // 2
    half = L // 2
    sec = lax.axis_index("section")
    me = lax.axis_index("tensor")

    def ring(pos):
        upper = pos // (T // 2)
        return (1 - upper) * (2 * pos) + upper * (2 * (T - 1 - pos) + 1)

    y = me % 2
    p = (1 - y) * (me // 2) + y * (T - 1 - me // 2)

    def at(offset):
        return ring((p + offset + 2 * T) % T)

    sides = (at(1), at(-1))
    signs = (1, -1)
    following = (sec + 1) % S
    previous = (sec + S - 1) % S

    def block(owner):
        return pl.ds(pl.multiple_of(owner * B, B), B)

    def ow_copy(owner):
        return pltpu.make_async_copy(ow_hbm.at[:, block(owner)], ow.at[:, block(owner)], ow_sem.at[owner])

    ctx_load = pltpu.make_async_copy(ctx_hbm, ctx, load_sem.at[2])
    ctx_load.start()
    ow_copy(at(H)).start()
    ow_copy(at(H - 1)).start()
    ow_copy(at(1 - H)).start()

    def load_rest(j, c):
        ow_copy(at(j)).start()
        return c

    def wait_rest(j, c):
        ow_copy(at(j)).wait()
        return c

    lax.fori_loop(T + 2 - H, T + H - 1, load_rest, 0)
    kv_load = pltpu.make_async_copy(kvw_hbm, kvw, load_sem.at[0])
    kv_load.start()
    q_load = pltpu.make_async_copy(qw_hbm, w.at[:, pl.ds(0, HD)], load_sem.at[1])
    q_load.start()

    gain_load = pltpu.make_async_copy(gain_hbm, gains.at[me], load_sem.at[3])
    gain_load.start()
    res_load = pltpu.make_async_copy(res_hbm, res, load_sem.at[4])
    res_load.start()
    table_loads = [
        pltpu.make_async_copy(source, target, load_sem.at[5 + i])
        for i, (source, target) in enumerate(
            ((cos_q_hbm, cos_q), (sin_q_hbm, sin_q), (cos_k_hbm, cos_k), (sin_k_hbm, sin_k))
        )
    ]
    for load in table_loads:
        load.start()

    barrier = pltpu.get_barrier_semaphore()

    def each_peer(act):
        def step(j, c):
            act((me + j) % T)
            return c

        lax.fori_loop(1, T, step, 0)

    def greet(s, t):
        pl.semaphore_signal(barrier, inc=1, device_id=(s, t), device_id_type=MESH)

    each_peer(lambda peer: greet(sec, peer))
    for section in (following, previous):
        greet(section, me)
        for side in range(2):
            greet(section, sides[side])

    def rows(g):
        return pl.ds(g * R, R)

    def is_long(side, g):
        return (g // (NG // 2)) == side

    order = [g for j in range(NG // 2) for g in (j, j + NG // 2)]
    pairs_of = [(side, g) for g in order for side in range(2)]
    longs = [pair for pair in pairs_of if is_long(*pair)]
    shorts = [pair for pair in pairs_of if not is_long(*pair)]

    def rs_copy(side, g, left, source, section=None):
        return pltpu.make_async_remote_copy(
            src_ref=source, dst_ref=rs.at[side, left - 1, rows(g)],
            send_sem=rs_send.at[side, g, left - 1], recv_sem=rs_recv.at[side, g, left - 1],
            device_id=(sec if section is None else section, sides[side]), device_id_type=MESH,
        )

    def shift_copy(g):
        return pltpu.make_async_remote_copy(
            src_ref=hand.at[rows(g)], dst_ref=base.at[rows(g)], send_sem=sh_send.at[g], recv_sem=sh_recv.at[g],
            device_id=(following, me), device_id_type=MESH,
        )

    def ag_copy(side, g, k, owner):
        return pltpu.make_async_remote_copy(
            src_ref=xb.at[owner, rows(g)], dst_ref=xb.at[owner, rows(g)],
            send_sem=ag_send.at[side, g, k], recv_sem=ag_recv.at[side, g, k],
            device_id=(sec, sides[side]), device_id_type=MESH,
        )

    def gain_copy(peer, slot):
        return pltpu.make_async_remote_copy(
            src_ref=gains.at[me], dst_ref=gains.at[slot], send_sem=g_send.at[peer], recv_sem=g_recv.at[slot],
            device_id=(sec, peer), device_id_type=MESH,
        )

    def kv_copy(peer, slot):
        return pltpu.make_async_remote_copy(
            src_ref=kvall.at[me], dst_ref=kvall.at[slot], send_sem=kv_send.at[peer], recv_sem=kv_recv.at[slot],
            device_id=(sec, peer), device_id_type=MESH,
        )

    def half_rows(side):
        return pl.ds(side * half, half)

    def term(owner):
        return jnp.dot(ctx[...], ow[:, block(owner)], preferred_element_type=F32)

    def project(owner):
        features = xb[owner].astype(F32)
        scaled = (features * gains[owner]).astype(BF16)
        squares = features * features
        total = squares[:, :HD]
        for i in range(1, B // HD):
            total = total + squares[:, i * HD:(i + 1) * HD]
        ssq[...] += total
        acc[...] += jnp.dot(scaled, w[block(owner), :], preferred_element_type=F32)

    def place(i):
        w[block(i), HD:] = jnp.concatenate(
            [jnp.transpose(kvw[:, block(i)]), jnp.zeros((B, HD - KC), BF16)], axis=1
        )

    ctx_load.wait()
    ow_copy(at(H)).wait()
    first[...] = term(at(H)).astype(BF16)
    pl.semaphore_wait(barrier, T + 5)
    for side, g in pairs_of:
        if is_long(side, g):
            rs_copy(side, g, H, first.at[rows(g)]).start()

    for side in range(2):
        ow_copy(at(signs[side] * (H - 1))).wait()
        terms[side] = term(at(signs[side] * (H - 1)))
    for side, g in pairs_of:
        if not is_long(side, g):
            rs[side, H - 1, rows(g), :] = terms[side, rows(g), :].astype(BF16)
            rs_copy(side, g, H - 1, rs.at[side, H - 1, rows(g)]).start()
    gain_load.wait()
    each_peer(lambda peer: gain_copy(peer, me).start())

    for side, g in pairs_of:
        if is_long(side, g):
            rs_copy(side, g, H, first.at[rows(g)]).wait_recv()
            total = rs[side, H - 1, rows(g), :].astype(F32) + terms[side, rows(g), :]
            rs[side, H - 1, rows(g), :] = total.astype(BF16)
            rs_copy(side, g, H - 1, rs.at[side, H - 1, rows(g)]).start()

    lax.fori_loop(T + 2 - H, T + H - 1, wait_rest, 0)
    for side in range(2):
        terms[side] = term(at(signs[side] * (H - 2)))
    res_load.wait()
    hand[...] = (term(me) + res[...].astype(F32)).astype(BF16)
    for g in order:
        shift_copy(g).start()
    acc[...] = jnp.zeros_like(acc)
    ssq[...] = jnp.zeros_like(ssq)
    kv_load.wait()
    place(T - 2)
    place(T - 1)

    def pass_sums(left, section=None):
        for side, g in shorts + longs:
            rs_copy(side, g, left + 1, first.at[rows(g)]).wait_recv()
            total = rs[side, left, rows(g), :].astype(F32) + terms[side, rows(g), :]
            rs[side, left, rows(g), :] = total.astype(BF16)
            rs_copy(side, g, left, rs.at[side, left, rows(g)], section).start()

    def reduce_step(i, c):
        left = H - 2 - i
        pass_sums(left)
        for side in range(2):
            terms[side] = term(at(signs[side] * (left - 1)))
        for n in range(2):
            place(2 * i + n)
        return c

    lax.fori_loop(0, H - 3, reduce_step, 0)
    pass_sums(1, following)
    for i in range(T - 6, T - 2):
        place(i)

    each_peer(lambda peer: gain_copy(peer, peer).wait_recv())
    q_load.wait()
    for load in table_loads:
        load.wait()
    for g in order:
        shift_copy(g).wait_recv()
        for side in range(2):
            rs_copy(side, g, 1, first.at[rows(g)], following).wait_recv()
        total = base[rows(g), :].astype(F32) + rs[0, 0, rows(g), :].astype(F32) + rs[1, 0, rows(g), :].astype(F32)
        xb[me, rows(g), :] = total.astype(BF16)
        for side in range(2):
            if is_long(side, g):
                ag_copy(side, g, 0, me).start()
    for side, g in shorts:
        ag_copy(side, g, 0, me).start()
    project(me)

    def gather_step(k, c):
        owners = [at(-signs[side] * (1 + k)) for side in range(2)]
        for side, g in longs + shorts:
            ag_copy(side, g, k, owners[side]).wait_recv()
            ag_copy(side, g, k + 1, owners[side]).start()
        for side in range(2):
            project(owners[side])
        return c

    lax.fori_loop(0, H - 2, gather_step, 0)
    owners = [at(-signs[side] * (H - 1)) for side in range(2)]
    for wanted in (True, False):
        for side, g in pairs_of:
            if is_long(side, g) == wanted:
                ag_copy(side, g, H - 2, owners[side]).wait_recv()
                if wanted:
                    ag_copy(side, g, H - 1, owners[side]).start()
    for side in range(2):
        project(owners[side])
    for side, g in pairs_of:
        if is_long(side, g):
            ag_copy(side, g, H - 1, at(H)).wait_recv()
    project(at(H))

    factor = lax.rsqrt(jnp.sum(ssq[...], axis=1, keepdims=True) * (1.0 / D) + EPS)
    pairs = (acc[:, HD:] * factor).astype(BF16)
    eye = lax.broadcasted_iota(jnp.int32, (KC, HD), 0) == lax.broadcasted_iota(jnp.int32, (KC, HD), 1)
    kvall[me] = dot_nt(eye.astype(F32).astype(BF16), pairs).astype(BF16)
    each_peer(lambda peer: kv_copy(peer, me).start())

    queries = acc[:, :HD] * factor
    turned = jnp.concatenate([queries[:, HD // 2:], queries[:, :HD // 2]], axis=1)
    queries = (queries * cos_q[...] + turned * sin_q[...]).astype(BF16)

    share = HD // T
    shift = share.bit_length() - 1
    feature = lax.broadcasted_iota(jnp.int32, (HD, T * KC), 0)
    column = lax.broadcasted_iota(jnp.int32, (HD, T * KC), 1)
    source = (feature >> shift) * KC + (feature & (share - 1)) + (me // GROUP) * (2 * share)
    key_picks = (column == source).astype(F32).astype(BF16)
    value_picks = (column == source + share).astype(F32).astype(BF16)

    each_peer(lambda peer: kv_copy(peer, peer).wait_recv())
    everything = kvall[...].reshape(T * KC, L)
    keys = jnp.dot(key_picks, everything, preferred_element_type=F32)
    values = jnp.dot(value_picks, everything, preferred_element_type=F32).astype(BF16)
    turned = jnp.concatenate([keys[HD // 2:], keys[:HD // 2]], axis=0)
    keys = (keys * cos_k[...] + turned * sin_k[...]).astype(BF16)
    for c in range(2):
        seen = (c + 1) * half
        scores = jnp.dot(queries[c * half:seen], keys[:, :seen], preferred_element_type=F32) * (HD ** -0.5)
        before = lax.broadcasted_iota(jnp.int32, (half, seen), 0) + c * half >= lax.broadcasted_iota(
            jnp.int32, (half, seen), 1
        )
        scores = jnp.where(before, scores, -1e30)
        weights = jnp.exp(scores - jnp.max(scores, axis=1, keepdims=True))
        weights = (weights * (1.0 / jnp.sum(weights, axis=1, keepdims=True))).astype(BF16)
        out[half_rows(c), :] = dot_nt(weights, values[:, :seen]).astype(BF16)

    def drain(k, c):
        for side, g in pairs_of:
            rs_copy(side, g, k + 1, first.at[rows(g)]).wait_send()
            ag_copy(side, g, k, me).wait_send()
        return c

    lax.fori_loop(0, H - 1, drain, 0)
    for side, g in pairs_of:
        if is_long(side, g):
            rs_copy(side, g, H, first.at[rows(g)]).wait_send()
            ag_copy(side, g, H - 1, me).wait_send()
    for g in range(NG):
        shift_copy(g).wait_send()
    each_peer(lambda peer: gain_copy(peer, me).wait_send())
    each_peer(lambda peer: kv_copy(peer, me).wait_send())


def on_device(context, out_weight, residual, gain, q_weight, kv_weight):
    T = lax.axis_size("tensor")
    S = lax.axis_size("section")
    _, L, HD = context.shape
    B = residual.shape[2]
    D = out_weight.shape[2]
    KC = kv_weight.shape[2]
    tables = rope_tables(L, HD)
    vmem = pl.BlockSpec(memory_space=pltpu.VMEM)
    hbm = pl.BlockSpec(memory_space=pltpu.HBM)
    dma = pltpu.SemaphoreType.DMA
    attended = pl.pallas_call(
        functools.partial(kernel, T, S),
        out_shape=jax.ShapeDtypeStruct((L, HD), BF16),
        in_specs=[hbm] * 10,
        out_specs=vmem,
        scratch_shapes=[
            pltpu.VMEM((L, HD), BF16),
            pltpu.VMEM((L, B), BF16),
            pltpu.VMEM((L, HD), F32),
            pltpu.VMEM((L, HD), F32),
            pltpu.VMEM((HD, L), F32),
            pltpu.VMEM((HD, L), F32),
            pltpu.VMEM((HD, D), BF16),
            pltpu.VMEM((KC, D), BF16),
            pltpu.VMEM((D, 2 * HD), BF16),
            pltpu.VMEM((L, B), BF16),
            pltpu.VMEM((2, T // 2, L, B), BF16),
            pltpu.VMEM((L, B), BF16),
            pltpu.VMEM((L, B), BF16),
            pltpu.VMEM((T, L, B), BF16),
            pltpu.VMEM((T, 1, B), F32),
            pltpu.VMEM((L, 2 * HD), F32),
            pltpu.VMEM((L, HD), F32),
            pltpu.VMEM((T, KC, L), BF16),
            pltpu.VMEM((2, L, B), F32),
            dma((T,)), dma((9,)),
            dma((2, NG, T // 2)), dma((2, NG, T // 2)),
            dma((NG,)), dma((NG,)),
            dma((2, NG, T // 2)), dma((2, NG, T // 2)),
            dma((T,)), dma((T,)),
            dma((T,)), dma((T,)),
        ],
        compiler_params=pltpu.CompilerParams(
            collective_id=0, has_side_effects=True, vmem_limit_bytes=62 * 2**20
        ),
        cost_estimate=pl.CostEstimate(
            flops=2 * L * D * HD * 3, bytes_accessed=D * HD * 6, transcendentals=L * L
        ),
        name="handover_attention",
    )(
        context[0], residual[0], gain, *[jnp.asarray(t) for t in tables],
        out_weight[0], q_weight[0], jnp.swapaxes(kv_weight[0], 0, 1),
    )
    return attended[None]


def solution(mesh):
    placed = (
        P("section", None, "tensor"),
        P("section", "tensor", None),
        P("section", None, "tensor"),
        P("section", "tensor"),
        P("section", None, "tensor"),
        P("section", None, "tensor"),
    )
    return jax.shard_map(
        on_device,
        mesh=mesh,
        in_specs=placed,
        out_specs=P("section", None, "tensor"),
        check_vma=False,
    )
```

```python
import functools

import jax
import jax.numpy as jnp
import numpy as np
from jax import lax
from jax.experimental import pallas as pl
from jax.experimental.pallas import tpu as pltpu
from jax.sharding import PartitionSpec as P

GROUP = 8
THETA = 500000.0
EPS = 1e-05
MESH = pl.DeviceIdType.MESH
BF16 = jnp.bfloat16
F32 = jnp.float32
NG = 8


def rope_tables(length, head_size):
    half = head_size // 2
    frequency = np.float32(THETA) ** (-(np.arange(half, dtype=np.float32) * np.float32(2.0) / np.float32(head_size)))
    angles = np.arange(length, dtype=np.float32)[:, None] * frequency.astype(np.float32)[None, :]
    cosine, sine = np.cos(angles).astype(np.float32), np.sin(angles).astype(np.float32)
    return (
        np.concatenate([cosine, cosine], axis=1),
        np.concatenate([-sine, sine], axis=1),
        np.ascontiguousarray(np.concatenate([cosine, cosine], axis=1).T),
        np.ascontiguousarray(np.concatenate([-sine, sine], axis=1).T),
    )


def dot_nt(a, b):
    return lax.dot_general(a, b, (((1,), (1,)), ((), ())), preferred_element_type=F32)


def kernel(
    T, S,
    ctx_hbm, res_hbm, gain_hbm, cos_q_hbm, sin_q_hbm, cos_k_hbm, sin_k_hbm, ow_hbm, qw_hbm, kvw_hbm,
    out,
    ctx, res, cos_q, sin_q, cos_k, sin_k,
    ow, kvw, w, first, rs, hand, base, xb, gains, acc, ssq, kvall, terms,
    ow_sem, load_sem, rs_send, rs_recv, sh_send, sh_recv, ag_send, ag_recv, g_send, g_recv, kv_send, kv_recv,
):
    L, HD = ctx.shape
    B = res.shape[1]
    D = ow.shape[1]
    KC = kvw.shape[0]
    R = L // NG
    H = T // 2
    half = L // 2
    sec = lax.axis_index("section")
    me = lax.axis_index("tensor")

    def ring(pos):
        upper = pos // (T // 2)
        return (1 - upper) * (2 * pos) + upper * (2 * (T - 1 - pos) + 1)

    y = me % 2
    p = (1 - y) * (me // 2) + y * (T - 1 - me // 2)

    def at(offset):
        return ring((p + offset + 2 * T) % T)

    sides = (at(1), at(-1))
    signs = (1, -1)
    following = (sec + 1) % S
    previous = (sec + S - 1) % S

    def block(owner):
        return pl.ds(pl.multiple_of(owner * B, B), B)

    def ow_copy(owner):
        return pltpu.make_async_copy(ow_hbm.at[:, block(owner)], ow.at[:, block(owner)], ow_sem.at[owner])

    ctx_load = pltpu.make_async_copy(ctx_hbm, ctx, load_sem.at[2])
    ctx_load.start()
    ow_copy(at(H)).start()
    ow_copy(at(H - 1)).start()
    ow_copy(at(1 - H)).start()

    def load_rest(j, c):
        ow_copy(at(j)).start()
        return c

    def wait_rest(j, c):
        ow_copy(at(j)).wait()
        return c

    lax.fori_loop(T + 2 - H, T + H - 1, load_rest, 0)
    kv_load = pltpu.make_async_copy(kvw_hbm, kvw, load_sem.at[0])
    kv_load.start()
    q_load = pltpu.make_async_copy(qw_hbm, w.at[:, pl.ds(0, HD)], load_sem.at[1])
    q_load.start()

    gain_load = pltpu.make_async_copy(gain_hbm, gains.at[me], load_sem.at[3])
    gain_load.start()
    res_load = pltpu.make_async_copy(res_hbm, res, load_sem.at[4])
    res_load.start()
    table_loads = [
        pltpu.make_async_copy(source, target, load_sem.at[5 + i])
        for i, (source, target) in enumerate(
            ((cos_q_hbm, cos_q), (sin_q_hbm, sin_q), (cos_k_hbm, cos_k), (sin_k_hbm, sin_k))
        )
    ]
    for load in table_loads:
        load.start()

    barrier = pltpu.get_barrier_semaphore()

    def each_peer(act):
        def step(j, c):
            act((me + j) % T)
            return c

        lax.fori_loop(1, T, step, 0)

    def greet(s, t):
        pl.semaphore_signal(barrier, inc=1, device_id=(s, t), device_id_type=MESH)

    each_peer(lambda peer: greet(sec, peer))
    for section in (following, previous):
        greet(section, me)
        for side in range(2):
            greet(section, sides[side])

    def rows(g):
        return pl.ds(g * R, R)

    def is_long(side, g):
        return (g // (NG // 2)) == side

    order = [g for j in range(NG // 2) for g in (j, j + NG // 2)]
    pairs_of = [(side, g) for g in order for side in range(2)]
    longs = [pair for pair in pairs_of if is_long(*pair)]
    shorts = [pair for pair in pairs_of if not is_long(*pair)]

    def rs_copy(side, g, left, source, section=None):
        return pltpu.make_async_remote_copy(
            src_ref=source, dst_ref=rs.at[side, left - 1, rows(g)],
            send_sem=rs_send.at[side, g, left - 1], recv_sem=rs_recv.at[side, g, left - 1],
            device_id=(sec if section is None else section, sides[side]), device_id_type=MESH,
        )

    def shift_copy(g):
        return pltpu.make_async_remote_copy(
            src_ref=hand.at[rows(g)], dst_ref=base.at[rows(g)], send_sem=sh_send.at[g], recv_sem=sh_recv.at[g],
            device_id=(following, me), device_id_type=MESH,
        )

    def ag_copy(side, g, k, owner):
        return pltpu.make_async_remote_copy(
            src_ref=xb.at[owner, rows(g)], dst_ref=xb.at[owner, rows(g)],
            send_sem=ag_send.at[side, g, k], recv_sem=ag_recv.at[side, g, k],
            device_id=(sec, sides[side]), device_id_type=MESH,
        )

    def gain_copy(peer, slot):
        return pltpu.make_async_remote_copy(
            src_ref=gains.at[me], dst_ref=gains.at[slot], send_sem=g_send.at[peer], recv_sem=g_recv.at[slot],
            device_id=(sec, peer), device_id_type=MESH,
        )

    def kv_copy(peer, slot):
        return pltpu.make_async_remote_copy(
            src_ref=kvall.at[me], dst_ref=kvall.at[slot], send_sem=kv_send.at[peer], recv_sem=kv_recv.at[slot],
            device_id=(sec, peer), device_id_type=MESH,
        )

    def half_rows(side):
        return pl.ds(side * half, half)

    def term(owner):
        return jnp.dot(ctx[...], ow[:, block(owner)], preferred_element_type=F32)

    def project(owner):
        features = xb[owner].astype(F32)
        scaled = (features * gains[owner]).astype(BF16)
        squares = features * features
        total = squares[:, :HD]
        for i in range(1, B // HD):
            total = total + squares[:, i * HD:(i + 1) * HD]
        ssq[...] += total
        acc[...] += jnp.dot(scaled, w[block(owner), :], preferred_element_type=F32)

    def place(i):
        w[block(i), HD:] = jnp.concatenate(
            [jnp.transpose(kvw[:, block(i)]), jnp.zeros((B, HD - KC), BF16)], axis=1
        )

    ctx_load.wait()
    ow_copy(at(H)).wait()
    first[...] = term(at(H)).astype(BF16)
    pl.semaphore_wait(barrier, T + 5)
    for side, g in pairs_of:
        if is_long(side, g):
            rs_copy(side, g, H, first.at[rows(g)]).start()

    for side in range(2):
        ow_copy(at(signs[side] * (H - 1))).wait()
        terms[side] = term(at(signs[side] * (H - 1)))
    for side, g in pairs_of:
        if not is_long(side, g):
            rs[side, H - 1, rows(g), :] = terms[side, rows(g), :].astype(BF16)
            rs_copy(side, g, H - 1, rs.at[side, H - 1, rows(g)]).start()
    gain_load.wait()
    each_peer(lambda peer: gain_copy(peer, me).start())

    for side, g in pairs_of:
        if is_long(side, g):
            rs_copy(side, g, H, first.at[rows(g)]).wait_recv()
            total = rs[side, H - 1, rows(g), :].astype(F32) + terms[side, rows(g), :]
            rs[side, H - 1, rows(g), :] = total.astype(BF16)
            rs_copy(side, g, H - 1, rs.at[side, H - 1, rows(g)]).start()

    lax.fori_loop(T + 2 - H, T + H - 1, wait_rest, 0)
    for side in range(2):
        terms[side] = term(at(signs[side] * (H - 2)))
    res_load.wait()
    hand[...] = (term(me) + res[...].astype(F32)).astype(BF16)
    for g in order:
        shift_copy(g).start()
    acc[...] = jnp.zeros_like(acc)
    ssq[...] = jnp.zeros_like(ssq)
    kv_load.wait()
    place(T - 2)
    place(T - 1)

    def pass_sums(left, section=None):
        for side, g in shorts + longs:
            rs_copy(side, g, left + 1, first.at[rows(g)]).wait_recv()
            total = rs[side, left, rows(g), :].astype(F32) + terms[side, rows(g), :]
            rs[side, left, rows(g), :] = total.astype(BF16)
            rs_copy(side, g, left, rs.at[side, left, rows(g)], section).start()

    def reduce_step(i, c):
        left = H - 2 - i
        pass_sums(left)
        for side in range(2):
            terms[side] = term(at(signs[side] * (left - 1)))
        for n in range(2):
            place(2 * i + n)
        return c

    lax.fori_loop(0, H - 3, reduce_step, 0)
    pass_sums(1, following)
    for i in range(T - 6, T - 2):
        place(i)

    each_peer(lambda peer: gain_copy(peer, peer).wait_recv())
    q_load.wait()
    for load in table_loads:
        load.wait()
    for g in order:
        shift_copy(g).wait_recv()
        for side in range(2):
            rs_copy(side, g, 1, first.at[rows(g)], following).wait_recv()
        total = base[rows(g), :].astype(F32) + rs[0, 0, rows(g), :].astype(F32) + rs[1, 0, rows(g), :].astype(F32)
        xb[me, rows(g), :] = total.astype(BF16)
        for side in range(2):
            if is_long(side, g):
                ag_copy(side, g, 0, me).start()
    for side, g in shorts:
        ag_copy(side, g, 0, me).start()
    project(me)

    def gather_step(k, c):
        owners = [at(-signs[side] * (1 + k)) for side in range(2)]
        for side, g in longs + shorts:
            ag_copy(side, g, k, owners[side]).wait_recv()
            ag_copy(side, g, k + 1, owners[side]).start()
        for side in range(2):
            project(owners[side])
        return c

    lax.fori_loop(0, H - 2, gather_step, 0)
    owners = [at(-signs[side] * (H - 1)) for side in range(2)]
    for wanted in (True, False):
        for side, g in pairs_of:
            if is_long(side, g) == wanted:
                ag_copy(side, g, H - 2, owners[side]).wait_recv()
                if wanted:
                    ag_copy(side, g, H - 1, owners[side]).start()
    for side in range(2):
        project(owners[side])
    for side, g in pairs_of:
        if is_long(side, g):
            ag_copy(side, g, H - 1, at(H)).wait_recv()
    project(at(H))

    factor = lax.rsqrt(jnp.sum(ssq[...], axis=1, keepdims=True) * (1.0 / D) + EPS)
    pairs = (acc[:, HD:] * factor).astype(BF16)
    eye = lax.broadcasted_iota(jnp.int32, (KC, HD), 0) == lax.broadcasted_iota(jnp.int32, (KC, HD), 1)
    kvall[me] = dot_nt(eye.astype(F32).astype(BF16), pairs).astype(BF16)
    each_peer(lambda peer: kv_copy(peer, me).start())

    queries = acc[:, :HD] * factor
    turned = jnp.concatenate([queries[:, HD // 2:], queries[:, :HD // 2]], axis=1)
    queries = (queries * cos_q[...] + turned * sin_q[...]).astype(BF16)

    share = HD // T
    shift = share.bit_length() - 1
    feature = lax.broadcasted_iota(jnp.int32, (HD, T * KC), 0)
    column = lax.broadcasted_iota(jnp.int32, (HD, T * KC), 1)
    source = (feature >> shift) * KC + (feature & (share - 1)) + (me // GROUP) * (2 * share)
    key_picks = (column == source).astype(F32).astype(BF16)
    value_picks = (column == source + share).astype(F32).astype(BF16)

    each_peer(lambda peer: kv_copy(peer, peer).wait_recv())
    everything = kvall[...].reshape(T * KC, L)
    keys = jnp.dot(key_picks, everything, preferred_element_type=F32)
    values = jnp.dot(value_picks, everything, preferred_element_type=F32).astype(BF16)
    turned = jnp.concatenate([keys[HD // 2:], keys[:HD // 2]], axis=0)
    keys = (keys * cos_k[...] + turned * sin_k[...]).astype(BF16)
    for c in range(2):
        seen = (c + 1) * half
        scores = jnp.dot(queries[c * half:seen], keys[:, :seen], preferred_element_type=F32) * (HD ** -0.5)
        before = lax.broadcasted_iota(jnp.int32, (half, seen), 0) + c * half >= lax.broadcasted_iota(
            jnp.int32, (half, seen), 1
        )
        scores = jnp.where(before, scores, -1e30)
        weights = jnp.exp(scores - jnp.max(scores, axis=1, keepdims=True))
        weights = (weights * (1.0 / jnp.sum(weights, axis=1, keepdims=True))).astype(BF16)
        out[half_rows(c), :] = dot_nt(weights, values[:, :seen]).astype(BF16)

    def drain(k, c):
        for side, g in pairs_of:
            rs_copy(side, g, k + 1, first.at[rows(g)]).wait_send()
            ag_copy(side, g, k, me).wait_send()
        return c

    lax.fori_loop(0, H - 1, drain, 0)
    for side, g in pairs_of:
        if is_long(side, g):
            rs_copy(side, g, H, first.at[rows(g)]).wait_send()
            ag_copy(side, g, H - 1, me).wait_send()
    for g in range(NG):
        shift_copy(g).wait_send()
    each_peer(lambda peer: gain_copy(peer, me).wait_send())
    each_peer(lambda peer: kv_copy(peer, me).wait_send())


def on_device(context, out_weight, residual, gain, q_weight, kv_weight):
    T = lax.axis_size("tensor")
    S = lax.axis_size("section")
    _, L, HD = context.shape
    B = residual.shape[2]
    D = out_weight.shape[2]
    KC = kv_weight.shape[2]
    tables = rope_tables(L, HD)
    vmem = pl.BlockSpec(memory_space=pltpu.VMEM)
    hbm = pl.BlockSpec(memory_space=pltpu.HBM)
    dma = pltpu.SemaphoreType.DMA
    attended = pl.pallas_call(
        functools.partial(kernel, T, S),
        out_shape=jax.ShapeDtypeStruct((L, HD), BF16),
        in_specs=[hbm] * 10,
        out_specs=vmem,
        scratch_shapes=[
            pltpu.VMEM((L, HD), BF16),
            pltpu.VMEM((L, B), BF16),
            pltpu.VMEM((L, HD), F32),
            pltpu.VMEM((L, HD), F32),
            pltpu.VMEM((HD, L), F32),
            pltpu.VMEM((HD, L), F32),
            pltpu.VMEM((HD, D), BF16),
            pltpu.VMEM((KC, D), BF16),
            pltpu.VMEM((D, 2 * HD), BF16),
            pltpu.VMEM((L, B), BF16),
            pltpu.VMEM((2, T // 2, L, B), BF16),
            pltpu.VMEM((L, B), BF16),
            pltpu.VMEM((L, B), BF16),
            pltpu.VMEM((T, L, B), BF16),
            pltpu.VMEM((T, 1, B), F32),
            pltpu.VMEM((L, 2 * HD), F32),
            pltpu.VMEM((L, HD), F32),
            pltpu.VMEM((T, KC, L), BF16),
            pltpu.VMEM((2, L, B), F32),
            dma((T,)), dma((9,)),
            dma((2, NG, T // 2)), dma((2, NG, T // 2)),
            dma((NG,)), dma((NG,)),
            dma((2, NG, T // 2)), dma((2, NG, T // 2)),
            dma((T,)), dma((T,)),
            dma((T,)), dma((T,)),
        ],
        compiler_params=pltpu.CompilerParams(
            collective_id=0, has_side_effects=True, vmem_limit_bytes=62 * 2**20
        ),
        cost_estimate=pl.CostEstimate(
            flops=2 * L * D * HD * 3, bytes_accessed=D * HD * 6, transcendentals=L * L
        ),
        name="handover_attention",
    )(
        context[0], residual[0], gain, *[jnp.asarray(t) for t in tables],
        out_weight[0], q_weight[0], jnp.swapaxes(kv_weight[0], 0, 1),
    )
    return attended[None]


def solution(mesh):
    placed = (
        P("section", None, "tensor"),
        P("section", "tensor", None),
        P("section", None, "tensor"),
        P("section", "tensor"),
        P("section", None, "tensor"),
        P("section", None, "tensor"),
    )
    return jax.shard_map(
        on_device,
        mesh=mesh,
        in_specs=placed,
        out_specs=P("section", None, "tensor"),
        check_vma=False,
    )
```
